32 devices in a mesh: region: 4 (over x, core), sector: 8 (over z, y).
Axes of the slice: x: 2, y: 2, z: 4, core: 2. Of those that a mesh axis runs over, the one named last changes fastest.
Arguments:
- psi: bfloat16 [4, 8, 256, 256], P('region', 'sector'), may hold values from -12 to 12
- left_env: bfloat16 [4, 8, 18, 256, 256], P('region', 'sector'), may hold values from -4 to 4
- right_env: bfloat16 [4, 8, 18, 256, 256], P('region', 'sector'), may hold values from -4 to 4
- diagonal: bfloat16 [4, 8, 256, 256], P('region', 'sector'), may hold values from -2 to 0
- left_coeff: float32 [18, 18], replicated, may hold values from -2 to 2
- right_coeff: float32 [18, 18], replicated, may hold values from -2 to 2
- mpo_mask: int32 [18, 18], replicated, may hold values 0 or 1
- sector_target: int32 [8, 18], P('sector'), may hold values from 0 to 7
- block_size: int32 [8], P('sector'), may hold values from 128 to 256, as said below
Outputs:
- bond: bfloat16 [4, 8, 256, 256], P('region', 'sector')
- energy: float32 [4], P('region')
The draws below stay inside these ranges and needn't reach their ends.
Inputs may be any that keep to these rules, and one draw needn't show every extreme that they name: `block_size`: one sector block has all 256 rows live, and one has exactly 128.
All inputs are finite; a program needn't handle non-finite values.
Results may differ from the reference program's by a relative error of at most 0.017.
Values may be sent and summed in bfloat16 or wider, within the bound.
A program may use at most 64 MiB of HBM per device.

```python
import math
import jax
import jax.numpy as jnp
from jax import lax

BLK = 256
W = 18
ITERS = 2
NREG = 4
NSEC = 8


env_level = 0.6


def sector_scales(base, ratio):
    ramp = jnp.arange(NSEC, dtype=jnp.float32) / (NSEC - 1)
    return base * jnp.power(ratio, ramp)


def block_sizes(key):
    salted = jax.random.fold_in(key, 303)
    key_sizes, key_first, key_offset = jax.random.split(salted, 3)
    sizes = jax.random.randint(key_sizes, (NSEC,), BLK // 2, BLK + 1)
    first = jax.random.randint(key_first, (), 0, NSEC)
    second = (first + jax.random.randint(key_offset, (), 1, NSEC)) % NSEC
    places = jnp.arange(NSEC, dtype=jnp.int32)
    sizes = jnp.where(places == first, BLK, sizes)
    sizes = jnp.where(places == second, BLK // 2, sizes)
    return sizes.astype(jnp.int32)


def env_factor(key, base, ratio):
    scales = sector_scales(base, ratio)
    middle = jnp.sqrt(scales[0] * scales[-1])
    sizes = block_sizes(key).astype(jnp.float32)
    return (middle / scales) ** 2 * (BLK / sizes) * (env_level / jnp.sqrt(jnp.float32(BLK)))


def draw_env(key, salt):
    shape = (NREG, NSEC, W, BLK, BLK)
    salted = jax.random.fold_in(key, salt)
    factor = env_factor(key, 0.6, 3.0)
    values = jnp.clip(jax.random.normal(salted, shape, jnp.float32), -4.0, 4.0)
    return (values * factor[None, :, None, None, None]).astype(jnp.bfloat16)


def draw_psi(key, part):
    shape = (NREG, NSEC, BLK, BLK)
    scales = sector_scales(0.6, 3.0)
    values = jnp.clip(jax.random.normal(key, shape, jnp.float32), -5.0, 5.0)
    return (values * scales[None, :, None, None]).astype(jnp.bfloat16)


def draw_left_env(key, part):
    return draw_env(key, 101)


def draw_right_env(key, part):
    return draw_env(key, 202)


def draw_diagonal(key, part):
    shape = (NREG, NSEC, BLK, BLK)
    salted = jax.random.fold_in(key, 404)
    key_order, key_values = jax.random.split(salted)
    orders = jax.vmap(lambda one_key: jax.random.permutation(one_key, NSEC))(jax.random.split(key_order, NREG))
    lower = (orders < NSEC // 2)[:, :, None, None]
    spread = jax.random.uniform(key_values, shape, jnp.float32, 0.0, 1.0)
    low_band = -2.0 + spread
    high_band = -spread
    return jnp.where(lower, low_band, high_band).astype(jnp.bfloat16)


def draw_block_size(key, part):
    return block_sizes(key)


def place_ends(array, own_key, low, high):
    dims = array.shape
    index_at = [jax.random.randint(jax.random.fold_in(own_key, axis), (), 0, dims[axis]) for axis in range(len(dims))]
    array = array.at[tuple(index_at)].set(low)
    longest = dims.index(max(dims))
    index_at[longest] = (index_at[longest] + 1) % dims[longest]
    return array.at[tuple(index_at)].set(high)


def normal_values(own_key, extent, scale, bound, held_as=jnp.bfloat16):
    drawn = jax.random.normal(own_key, extent, jnp.float32) * scale
    return jnp.minimum(jnp.maximum(drawn, -bound), bound).astype(held_as)


def setup_inputs(seed: int = 0) -> dict:
    seeds = jax.random.split(jax.random.key(seed), 10)
    return {
        "psi": draw_psi(jax.random.fold_in(seeds[9], 71), 0),
        "left_env": draw_left_env(jax.random.fold_in(seeds[9], 71), 0),
        "right_env": draw_right_env(jax.random.fold_in(seeds[9], 71), 0),
        "diagonal": draw_diagonal(jax.random.fold_in(seeds[9], 71), 0),
        "left_coeff": normal_values(seeds[4], (W, W), (W // 2) ** -0.5, 2.0, jnp.float32),
        "right_coeff": normal_values(seeds[5], (W, W), (W // 2) ** -0.5, 2.0, jnp.float32),
        "mpo_mask": place_ends((jax.random.randint(seeds[6], (W, W), 0, 2) < 1).astype(jnp.int32), jax.random.fold_in(seeds[6], 1), 0, 1),
        "sector_target": place_ends(jax.random.randint(seeds[7], (NSEC, W), 0, NSEC), jax.random.fold_in(seeds[7], 1), 0, NSEC - 1).astype(jnp.int32),
        "block_size": draw_block_size(jax.random.fold_in(seeds[9], 71), 0),
    }


step_size = 0.5

def reference(psi, left_env, right_env, diagonal, left_coeff, right_coeff, mpo_mask, sector_target, block_size):
    highest = lax.Precision.HIGHEST
    positions = jnp.arange(BLK, dtype=jnp.int32)
    live_rows = positions[None, :] < block_size[:, None]
    keep_mask = (live_rows[:, :, None] & live_rows[:, None, :]).astype(jnp.float32)
    pattern = mpo_mask.astype(jnp.float32)
    left_mix = left_coeff * pattern
    right_mix = right_coeff * pattern
    routing = (sector_target[:, :, None] == jnp.arange(NSEC, dtype=jnp.int32)[None, None, :]).astype(jnp.float32)
    inv_root = 1.0 / math.sqrt(W)

    def prepare(items):
        psi_here, left_here, right_here = items
        masked = (psi_here.astype(jnp.float32) * keep_mask).astype(jnp.bfloat16)
        wide = masked.astype(jnp.float32)
        start_norm = jnp.sum(wide * wide)
        rescale = NSEC * BLK / start_norm
        left_half = jnp.einsum('swij,sjk->swik', left_here.astype(jnp.float32), wide).astype(jnp.bfloat16)
        left_terms = jnp.einsum('sji,swjk->swik', wide, left_half.astype(jnp.float32))
        left_out = (rescale * jnp.einsum('vw,swik->svik', left_mix, left_terms, precision=highest)).astype(jnp.bfloat16)
        right_half = jnp.einsum('swij,skj->swik', right_here.astype(jnp.float32), wide).astype(jnp.bfloat16)
        right_terms = jnp.einsum('sij,swjk->swik', wide, right_half.astype(jnp.float32))
        right_out = (rescale * jnp.einsum('vw,swik->svik', right_mix, right_terms, precision=highest)).astype(jnp.bfloat16)
        return (left_out, right_out, start_norm)
    left_out, right_out, start_norm = lax.map(prepare, (psi, left_env, right_env))

    def solve(index):
        psi_here = lax.dynamic_index_in_dim(psi, index, 0, keepdims=False)
        diag_here = lax.dynamic_index_in_dim(diagonal, index, 0, keepdims=False).astype(jnp.float32)
        before = jnp.maximum(index - 1, 0).astype(jnp.int32)
        after = jnp.minimum(index + 1, NREG - 1).astype(jnp.int32)
        left_used = jnp.where(index == 0, left_env[0], lax.dynamic_index_in_dim(left_out, before, 0, keepdims=False))
        right_used = jnp.where(index == NREG - 1, right_env[NREG - 1], lax.dynamic_index_in_dim(right_out, after, 0, keepdims=False))
        norm_here = lax.dynamic_index_in_dim(start_norm, index, 0, keepdims=False)
        masked = (psi_here.astype(jnp.float32) * keep_mask).astype(jnp.bfloat16)
        vector = (masked.astype(jnp.float32) * jnp.sqrt(NSEC * BLK * BLK / norm_here)).astype(jnp.bfloat16)
        energy = jnp.zeros((), jnp.float32)
        for step in range(ITERS):
            wide = vector.astype(jnp.float32)
            applied = jnp.einsum('swij,sjk->swik', left_used.astype(jnp.float32), wide).astype(jnp.bfloat16)
            product = jnp.einsum('swik,swkl->swil', applied.astype(jnp.float32), right_used.astype(jnp.float32))
            partial_value = jnp.einsum('swt,swil->stil', routing, product, precision=highest) * inv_root
            partial_value = lax.optimization_barrier(partial_value.astype(jnp.bfloat16)).astype(jnp.float32)
            applied_h = (lax.optimization_barrier(jnp.sum(partial_value, axis=0)) + diag_here * wide) * keep_mask
            intersection = jnp.sum(wide * wide)
            cross = jnp.sum(wide * applied_h)
            energy = cross / intersection
            update = wide - step_size * (applied_h - energy * wide)
            norm_sq = jnp.sum(update * update)
            vector = (update * jnp.sqrt(NSEC * BLK * BLK / norm_sq)).astype(jnp.bfloat16)
        return (vector, energy)
    bond, energy = lax.map(solve, jnp.arange(NREG, dtype=jnp.int32))
    return (bond, energy)
```

```python
import functools
import math

import jax
import jax.numpy as jnp
from jax import lax
from jax.experimental import pallas as pl
from jax.experimental.pallas import tpu as pltpu
from jax.sharding import PartitionSpec as P

ITERS = 2
STEP = 0.5
SLABS = 4
F32 = jnp.float32
BF16 = jnp.bfloat16
MESH = pl.DeviceIdType.MESH


def nn(a, b):
    return lax.dot_general(a, b, (((1,), (0,)), ((), ())), preferred_element_type=F32)


def nt(a, b):
    return lax.dot_general(a, b, (((1,), (1,)), ((), ())), preferred_element_type=F32)


def iota(shape, dim):
    return lax.broadcasted_iota(jnp.int32, shape, dim)


def total(x):
    return jnp.sum(jnp.sum(x, axis=0, keepdims=True), axis=1, keepdims=True)


def kernel(
    regions, ys, zs, width, terms,
    psi_ref, left_hbm, right_hbm, diag_ref, lc_ref, rc_ref, mask_ref, target_ref, size_ref,
    bond_ref, energy_ref,
    env, mixed, frame, out_slow, out_fast, slow, fast, vec, unit, route,
    term, part, y_in, zsum, z_in, result, scal,
    load_sem, slow_send, slow_recv, fast_sem, y_send, y_recv, z_send, z_recv, s_send, s_recv,
):
    sectors = ys * zs
    rows = width // SLABS
    cells = float(sectors * width * width)
    region = lax.axis_index("region")
    me = lax.axis_index("sector")
    my_y, my_z = lax.rem(me, ys), lax.div(me, ys)
    odd = lax.rem(region, 2)
    even = odd == 0
    fast_peer = region + 1 - 2 * odd
    slow_peer = region - 1 + 2 * odd
    inner = jnp.logical_and(slow_peer >= 0, slow_peer < regions)
    edge = jnp.logical_not(inner)

    barrier = pltpu.get_barrier_semaphore()
    for d in range(1, sectors):
        pl.semaphore_signal(
            barrier, inc=1, device_id={"sector": lax.rem(me + d, sectors)}, device_id_type=MESH
        )
    pl.semaphore_signal(barrier, inc=1, device_id={"region": fast_peer}, device_id_type=MESH)

    @pl.when(inner)
    def _():
        pl.semaphore_signal(barrier, inc=1, device_id={"region": slow_peer}, device_id_type=MESH)

    def load(source, slot):
        return pltpu.make_async_copy(source, env.at[slot], load_sem.at[slot])

    @pl.when(even)
    def _():
        load(right_hbm, 0).start()
        load(left_hbm, 1).start()

    @pl.when(jnp.logical_not(even))
    def _():
        load(left_hbm, 0).start()
        load(right_hbm, 1).start()

    size = size_ref[0]
    square = (width, width)
    keep = jnp.logical_and(iota(square, 0) < size, iota(square, 1) < size)
    unit[...] = jnp.where(iota(square, 0) == iota(square, 1), 1.0, 0.0).astype(BF16)
    wide = jnp.where(keep, psi_ref[...].astype(F32), 0.0)
    masked = wide.astype(BF16)
    turned = nt(unit[...], masked).astype(BF16)

    @pl.when(even)
    def _():
        frame[0] = masked
        frame[1] = turned

    @pl.when(jnp.logical_not(even))
    def _():
        frame[0] = turned
        frame[1] = masked

    lanes = iota((8, 128), 1)

    def scalar_copy(which, d):
        peer = lax.rem(me + d, sectors)
        return pltpu.make_async_remote_copy(
            src_ref=scal.at[which, me], dst_ref=scal.at[which, me],
            send_sem=s_send.at[which, d - 1], recv_sem=s_recv.at[which, d - 1],
            device_id={"sector": peer}, device_id_type=MESH,
        )

    def scalar_start(which, values):
        packed = jnp.zeros((8, 128), F32)
        for lane, value in enumerate(values):
            packed = jnp.where(lanes == lane, jnp.broadcast_to(value, (8, 128)), packed)
        scal[which, me] = packed
        for d in range(1, sectors):
            scalar_copy(which, d).start()

    def scalar_finish(which, count):
        for d in range(1, sectors):
            scalar_copy(which, d).wait_recv()
        added = jnp.sum(scal[which], axis=0)[0:1, :]
        return [
            jnp.sum(jnp.where(lanes[0:1] == lane, added, 0.0), axis=1, keepdims=True)
            for lane in range(count)
        ]

    pl.semaphore_wait(barrier, sectors + inner.astype(jnp.int32))

    scalar_start(0, [total(wide * wide)])

    tall = 8 * terms
    spread = jnp.where((iota((tall, terms), 0) >> 3) == iota((tall, terms), 1), 1.0, 0.0).astype(BF16)
    same = (iota((tall, tall), 0) & 7) == (iota((tall, tall), 1) & 7)
    pattern = mask_ref[...].astype(F32)

    def mixer(coeff):
        over = nn(spread, (coeff * pattern).astype(BF16)).astype(BF16)
        return jnp.where(same, nt(over, spread), 0.0).astype(BF16)

    left_c, right_c = lc_ref[...], rc_ref[...]
    parity = odd.astype(F32)
    mixers = [
        mixer(right_c + parity * (left_c - right_c)),
        mixer(left_c + parity * (right_c - left_c)),
    ]
    wanted = (sectors * 8, tall)
    aim = jnp.zeros(wanted, jnp.int32)
    for w in range(terms):
        aim = jnp.where((iota(wanted, 1) >> 3) == w, target_ref[0, w], aim)
    block = iota(wanted, 0) >> 3
    z_bits = zs.bit_length() - 1
    mine = (block & (zs - 1)) * ys + (block >> z_bits)
    hit = jnp.logical_and(aim == mine, (iota(wanted, 0) & 7) == (iota(wanted, 1) & 7))
    route[...] = jnp.where(hit, 1.0, 0.0).astype(BF16)

    def mix(slot):
        matrix = mixers[slot]

        def body(i, carry):
            start = pl.multiple_of(i * 16, 16)
            x = env[slot, :, pl.ds(start, 16), :].astype(F32)
            halves = []
            for h in range(2):
                piece = x[:, 8 * h : 8 * h + 8, :].reshape(tall, width).astype(BF16)
                halves.append(nn(matrix, piece).reshape(terms, 8, width))
            mixed[:, pl.ds(start, 16), :] = jnp.concatenate(halves, axis=1).astype(BF16)
            return carry

        lax.fori_loop(0, width // 16, body, 0)

    group = 3 if terms % 3 == 0 else (2 if terms % 2 == 0 else 1)

    def carry_env(slot, rescale, store):
        def body(i, carry):
            for j in range(group):
                v = i * group + j
                a = frame[slot]
                y = nn(a, mixed[v]).astype(BF16)
                first = jnp.where(even, a, y)
                second = jnp.where(even, y, a)
                store(v, (rescale * nt(first, second)).astype(BF16))
            return carry

        lax.fori_loop(0, terms // group, body, 0)

    def load_wait(slot):
        load(left_hbm, slot).wait()

    def slow_copy(k):
        return pltpu.make_async_remote_copy(
            src_ref=out_slow.at[k], dst_ref=slow.at[k],
            send_sem=slow_send.at[k], recv_sem=slow_recv.at[k],
            device_id={"region": slow_peer}, device_id_type=MESH,
        )

    fast_copy = pltpu.make_async_remote_copy(
        src_ref=out_fast, dst_ref=fast, send_sem=fast_sem.at[0], recv_sem=fast_sem.at[1],
        device_id={"region": fast_peer}, device_id_type=MESH,
    )

    load_wait(0)
    mix(0)
    (start_norm,) = scalar_finish(0, 1)
    rescale = sectors * width / start_norm

    def store_slow(v, value):
        for k in range(SLABS):
            out_slow[k, v] = value[k * rows : (k + 1) * rows]

    carry_env(0, rescale, store_slow)

    @pl.when(inner)
    def _():
        for k in range(min(2, SLABS)):
            slow_copy(k).start()

    load_wait(1)
    mix(1)

    def store_fast(v, value):
        out_fast[v] = value

    carry_env(1, rescale, store_fast)
    fast_copy.start()

    @pl.when(jnp.logical_and(edge, even))
    def _():
        def body(v, carry):
            for k in range(SLABS):
                slow[k, v] = env[1, v, k * rows : (k + 1) * rows, :]
            return carry

        lax.fori_loop(0, terms, body, 0)

    @pl.when(jnp.logical_and(edge, jnp.logical_not(even)))
    def _():
        def body(v, carry):
            value = nt(unit[...], env[1, v]).astype(BF16)
            for k in range(SLABS):
                slow[k, v] = value[k * rows : (k + 1) * rows]
            return carry

        lax.fori_loop(0, terms, body, 0)

    vec[0] = (frame[0].astype(F32) * jnp.sqrt(cells / start_norm)).astype(BF16)
    diag = diag_ref[...]
    diag_frame = jnp.where(even, diag, nt(unit[...], diag).astype(BF16))
    inv_root = 1.0 / math.sqrt(terms)

    def y_copy(it, k, d):
        peer_y = lax.rem(my_y + d, ys)
        return pltpu.make_async_remote_copy(
            src_ref=part.at[it, k, peer_y], dst_ref=y_in.at[it, k, d - 1],
            send_sem=y_send.at[it, k, d - 1], recv_sem=y_recv.at[it, k, d - 1],
            device_id={"sector": my_z * ys + peer_y}, device_id_type=MESH,
        )

    def z_copy(it, k, d):
        peer_z = lax.rem(my_z + d, zs)
        return pltpu.make_async_remote_copy(
            src_ref=zsum.at[it, k, peer_z], dst_ref=z_in.at[it, k, d - 1],
            send_sem=z_send.at[it, k, d - 1], recv_sem=z_recv.at[it, k, d - 1],
            device_id={"sector": peer_z * ys + my_y}, device_id_type=MESH,
        )

    def z_phase(it, k):
        for d in range(1, ys):
            y_copy(it, k, d).wait_recv()
        added = part[it, k, my_y].astype(F32)
        for d in range(1, ys):
            added = added + y_in[it, k, d - 1].astype(F32)
        zsum[it, k] = added.astype(BF16)
        for d in range(1, zs):
            z_copy(it, k, d).start()

    def apply(it):
        def body(k, carry):
            if it == 0:
                @pl.when(inner)
                def _():
                    slow_copy(k).wait_recv()

                @pl.when(jnp.logical_and(inner, k < SLABS - 2))
                def _():
                    slow_copy(k).wait_send()
                    slow_copy(k + 2).start()

            half = nn(slow[k].reshape(terms * rows, width), vec[it]).astype(BF16)
            for w in range(terms):
                term[w] = nn(half[w * rows : (w + 1) * rows], fast[w])
            matrix = route[...]
            for i in range(rows // 16):
                halves = []
                for h in range(2):
                    at = 16 * i + 8 * h
                    piece = term[:, at : at + 8, :].reshape(tall, width).astype(BF16)
                    halves.append((nn(matrix, piece) * inv_root).reshape(ys, zs, 8, width))
                part[it, k, :, :, 16 * i : 16 * i + 16, :] = jnp.concatenate(halves, axis=2).astype(BF16)
            for d in range(1, ys):
                y_copy(it, k, d).start()

            @pl.when(k >= 1)
            def _():
                z_phase(it, k - 1)

            return carry

        lax.fori_loop(0, SLABS, body, 0)
        z_phase(it, SLABS - 1)
        for k in range(SLABS):
            for d in range(1, zs):
                z_copy(it, k, d).wait_recv()
            added = zsum[it, k, my_z].astype(F32)
            for d in range(1, zs):
                added = added + z_in[it, k, d - 1].astype(F32)
            result[it, k * rows : (k + 1) * rows, :] = added
        source = vec[it].astype(F32)
        value = jnp.where(keep, result[it] + diag_frame.astype(F32) * source, 0.0)
        result[it] = value

    fast_copy.wait_recv()
    apply(0)
    first = result[0]
    vec[1] = first.astype(BF16)
    start = vec[0].astype(F32)
    scalar_start(1, [total(start * start), total(start * first), total(first * first)])
    apply(1)
    vv, vh, hh = scalar_finish(1, 3)
    energy = vh / vv
    near = 1.0 + STEP * energy
    scale = jnp.sqrt(cells / jnp.maximum(near * near * vv - 2.0 * STEP * near * vh + STEP * STEP * hh, vv))
    start = vec[0].astype(F32)
    first = result[0]
    x = scale * near * start - scale * STEP * first
    applied = scale * near * first - scale * STEP * result[1]
    y = applied - energy * x
    result[0] = x
    result[1] = y
    scalar_start(2, [total(x * x), total(x * y), total(y * y)])
    xx, xy, yy = scalar_finish(2, 3)
    gap = xy / xx
    norm = xx + STEP * STEP * jnp.maximum(yy - gap * xy, 0.0)
    grow = jnp.sqrt(cells / norm)
    bond = (grow * (result[0] - STEP * (result[1] - gap * result[0]))).astype(BF16)

    @pl.when(even)
    def _():
        bond_ref[...] = bond

    @pl.when(jnp.logical_not(even))
    def _():
        bond_ref[...] = nt(unit[...], bond).astype(BF16)

    energy_ref[...] = jnp.broadcast_to(energy + gap, (1, 128))

    for which in range(3):
        for d in range(1, sectors):
            scalar_copy(which, d).wait_send()
    fast_copy.wait_send()

    @pl.when(inner)
    def _():
        for k in range(max(0, SLABS - 2), SLABS):
            slow_copy(k).wait_send()

    for it in range(ITERS):
        for k in range(SLABS):
            for d in range(1, ys):
                y_copy(it, k, d).wait_send()
            for d in range(1, zs):
                z_copy(it, k, d).wait_send()


def local(regions, ys, zs, psi, left_env, right_env, diagonal, lc, rc, mask, target, size):
    width, terms = psi.shape[-1], left_env.shape[2]
    sectors, rows = ys * zs, width // SLABS
    envs = (terms, width, width)
    vmem = pl.BlockSpec(memory_space=pltpu.VMEM)
    smem = pl.BlockSpec(memory_space=pltpu.SMEM)
    hbm = pl.BlockSpec(memory_space=pl.ANY)
    dma = pltpu.SemaphoreType.DMA
    bond, energy = pl.pallas_call(
        functools.partial(kernel, regions, ys, zs, width, terms),
        out_shape=(
            jax.ShapeDtypeStruct((width, width), BF16),
            jax.ShapeDtypeStruct((1, 128), F32),
        ),
        in_specs=[vmem, hbm, hbm, vmem, vmem, vmem, vmem, smem, smem],
        out_specs=(vmem, vmem),
        scratch_shapes=[
            pltpu.VMEM((2,) + envs, BF16),
            pltpu.VMEM(envs, BF16),
            pltpu.VMEM((2, width, width), BF16),
            pltpu.VMEM((SLABS, terms, rows, width), BF16),
            pltpu.VMEM(envs, BF16),
            pltpu.VMEM((SLABS, terms, rows, width), BF16),
            pltpu.VMEM(envs, BF16),
            pltpu.VMEM((2, width, width), BF16),
            pltpu.VMEM((width, width), BF16),
            pltpu.VMEM((sectors * 8, terms * 8), BF16),
            pltpu.VMEM((terms, rows, width), F32),
            pltpu.VMEM((ITERS, SLABS, ys, zs, rows, width), BF16),
            pltpu.VMEM((ITERS, SLABS, max(ys - 1, 1), zs, rows, width), BF16),
            pltpu.VMEM((ITERS, SLABS, zs, rows, width), BF16),
            pltpu.VMEM((ITERS, SLABS, max(zs - 1, 1), rows, width), BF16),
            pltpu.VMEM((2, width, width), F32),
            pltpu.VMEM((3, sectors, 8, 128), F32),
            dma((2,)),
            dma((SLABS,)),
            dma((SLABS,)),
            dma((2,)),
            dma((ITERS, SLABS, max(ys - 1, 1))),
            dma((ITERS, SLABS, max(ys - 1, 1))),
            dma((ITERS, SLABS, max(zs - 1, 1))),
            dma((ITERS, SLABS, max(zs - 1, 1))),
            dma((3, sectors - 1)),
            dma((3, sectors - 1)),
        ],
        compiler_params=pltpu.CompilerParams(
            collective_id=0, has_side_effects=True, vmem_limit_bytes=56 * 2**20
        ),
    )(
        psi.reshape(width, width), left_env.reshape(envs), right_env.reshape(envs),
        diagonal.reshape(width, width), lc, rc, mask, target, size,
    )
    return bond.reshape(1, 1, width, width), energy[0, :1]


def solution(mesh):
    regions, sectors = mesh.shape["region"], mesh.shape["sector"]
    ys = 1
    while (2 * ys) * (2 * ys) * 2 <= sectors:
        ys *= 2
    in_specs = (
        P("region", "sector", None, None),
        P("region", "sector", None, None, None),
        P("region", "sector", None, None, None),
        P("region", "sector", None, None),
        P(),
        P(),
        P(),
        P("sector", None),
        P("sector"),
    )
    out_specs = (P("region", "sector", None, None), P("region"))
    body = functools.partial(local, regions, ys, sectors // ys)
    return jax.shard_map(body, mesh=mesh, in_specs=in_specs, out_specs=out_specs, check_vma=False)
```

```python
import functools
import math

import jax
import jax.numpy as jnp
from jax import lax
from jax.experimental import pallas as pl
from jax.experimental.pallas import tpu as pltpu
from jax.sharding import PartitionSpec as P

ITERS = 2
STEP = 0.5
SLABS = (8, 4)
AHEAD = 2
F32 = jnp.float32
BF16 = jnp.bfloat16
MESH = pl.DeviceIdType.MESH


def nn(a, b):
    return lax.dot_general(a, b, (((1,), (0,)), ((), ())), preferred_element_type=F32)


def nt(a, b):
    return lax.dot_general(a, b, (((1,), (1,)), ((), ())), preferred_element_type=F32)


def iota(shape, dim):
    return lax.broadcasted_iota(jnp.int32, shape, dim)


def total(x):
    return jnp.sum(jnp.sum(x, axis=0, keepdims=True), axis=1, keepdims=True)


def kernel(
    regions, ys, zs, width, terms,
    psi_ref, left_hbm, right_hbm, diag_ref, lc_ref, rc_ref, mask_ref, target_ref, size_ref,
    bond_ref, energy_ref,
    env, mixed, frame, out_slow, out_fast, slow, fast, vec, unit, route,
    term, part0, part1, y_in0, y_in1, zsum0, zsum1, z_in0, z_in1, result, scal,
    load_sem, slow_send, slow_recv, fast_sem, y_send, y_recv, z_send, z_recv, s_send, s_recv,
):
    sectors = ys * zs
    part, y_in = (part0, part1), (y_in0, y_in1)
    zsum, z_in = (zsum0, zsum1), (z_in0, z_in1)
    slabs = SLABS[0]
    rows = width // slabs
    cells = float(sectors * width * width)
    region = lax.axis_index("region")
    me = lax.axis_index("sector")
    my_y, my_z = lax.rem(me, ys), lax.div(me, ys)
    odd = lax.rem(region, 2)
    even = odd == 0
    fast_peer = region + 1 - 2 * odd
    slow_peer = region - 1 + 2 * odd
    inner = jnp.logical_and(slow_peer >= 0, slow_peer < regions)
    edge = jnp.logical_not(inner)

    barrier = pltpu.get_barrier_semaphore()
    for d in range(1, sectors):
        pl.semaphore_signal(
            barrier, inc=1, device_id={"sector": lax.rem(me + d, sectors)}, device_id_type=MESH
        )
    pl.semaphore_signal(barrier, inc=1, device_id={"region": fast_peer}, device_id_type=MESH)

    @pl.when(inner)
    def _():
        pl.semaphore_signal(barrier, inc=1, device_id={"region": slow_peer}, device_id_type=MESH)

    def load(source, slot):
        return pltpu.make_async_copy(source, env.at[slot], load_sem.at[slot])

    @pl.when(even)
    def _():
        load(right_hbm, 0).start()
        load(left_hbm, 1).start()

    @pl.when(jnp.logical_not(even))
    def _():
        load(left_hbm, 0).start()
        load(right_hbm, 1).start()

    size = size_ref[0]
    square = (width, width)
    keep = jnp.logical_and(iota(square, 0) < size, iota(square, 1) < size)
    unit[...] = jnp.where(iota(square, 0) == iota(square, 1), 1.0, 0.0).astype(BF16)
    wide = jnp.where(keep, psi_ref[...].astype(F32), 0.0)
    masked = wide.astype(BF16)
    turned = nt(unit[...], masked).astype(BF16)

    @pl.when(even)
    def _():
        frame[0] = masked
        frame[1] = turned

    @pl.when(jnp.logical_not(even))
    def _():
        frame[0] = turned
        frame[1] = masked

    lanes = iota((8, 128), 1)

    def scalar_copy(which, d):
        peer = lax.rem(me + d, sectors)
        return pltpu.make_async_remote_copy(
            src_ref=scal.at[which, me], dst_ref=scal.at[which, me],
            send_sem=s_send.at[which, d - 1], recv_sem=s_recv.at[which, d - 1],
            device_id={"sector": peer}, device_id_type=MESH,
        )

    def scalar_start(which, values):
        packed = jnp.zeros((8, 128), F32)
        for lane, value in enumerate(values):
            packed = jnp.where(lanes == lane, jnp.broadcast_to(value, (8, 128)), packed)
        scal[which, me] = packed
        for d in range(1, sectors):
            scalar_copy(which, d).start()

    def scalar_finish(which, count):
        for d in range(1, sectors):
            scalar_copy(which, d).wait_recv()
        added = jnp.sum(scal[which], axis=0)[0:1, :]
        return [
            jnp.sum(jnp.where(lanes[0:1] == lane, added, 0.0), axis=1, keepdims=True)
            for lane in range(count)
        ]

    pl.semaphore_wait(barrier, sectors + inner.astype(jnp.int32))

    scalar_start(0, [total(wide * wide)])

    tall = 8 * terms
    spread = jnp.where((iota((tall, terms), 0) >> 3) == iota((tall, terms), 1), 1.0, 0.0).astype(BF16)
    same = (iota((tall, tall), 0) & 7) == (iota((tall, tall), 1) & 7)
    pattern = mask_ref[...].astype(F32)

    def mixer(coeff):
        over = nn(spread, (coeff * pattern).astype(BF16)).astype(BF16)
        return jnp.where(same, nt(over, spread), 0.0).astype(BF16)

    left_c, right_c = lc_ref[...], rc_ref[...]
    parity = odd.astype(F32)
    mixers = [
        mixer(right_c + parity * (left_c - right_c)),
        mixer(left_c + parity * (right_c - left_c)),
    ]
    wanted = (sectors * 8, tall)
    aim = jnp.zeros(wanted, jnp.int32)
    for w in range(terms):
        aim = jnp.where((iota(wanted, 1) >> 3) == w, target_ref[0, w], aim)
    block = iota(wanted, 0) >> 3
    z_bits = zs.bit_length() - 1
    mine = (block & (zs - 1)) * ys + (block >> z_bits)
    hit = jnp.logical_and(aim == mine, (iota(wanted, 0) & 7) == (iota(wanted, 1) & 7))
    route[...] = jnp.where(hit, 1.0, 0.0).astype(BF16)

    def mix(slot):
        matrix = mixers[slot]

        def body(i, carry):
            for j in range(4):
                start = pl.multiple_of(i * 64 + j * 16, 16)
                x = env[slot, :, pl.ds(start, 16), :].astype(F32)
                halves = []
                for h in range(2):
                    piece = x[:, 8 * h : 8 * h + 8, :].reshape(tall, width).astype(BF16)
                    halves.append(nn(matrix, piece).reshape(terms, 8, width))
                mixed[:, pl.ds(start, 16), :] = jnp.concatenate(halves, axis=1).astype(BF16)
            return carry

        lax.fori_loop(0, width // 64, body, 0)

    group = max(g for g in range(1, 10) if terms % g == 0)

    def carry_env(slot, rescale, store):
        def body(i, carry):
            for j in range(group):
                v = i * group + j
                a = frame[slot]
                y = nn(a, mixed[v]).astype(BF16)
                first = jnp.where(even, a, y)
                second = jnp.where(even, y, a)
                store(v, (rescale * nt(first, second)).astype(BF16))
            return carry

        lax.fori_loop(0, terms // group, body, 0)

    def load_wait(slot):
        load(left_hbm, slot).wait()

    def slow_copy(k):
        return pltpu.make_async_remote_copy(
            src_ref=out_slow.at[k], dst_ref=slow.at[k],
            send_sem=slow_send.at[k], recv_sem=slow_recv.at[k],
            device_id={"region": slow_peer}, device_id_type=MESH,
        )

    fast_copy = pltpu.make_async_remote_copy(
        src_ref=out_fast, dst_ref=fast, send_sem=fast_sem.at[0], recv_sem=fast_sem.at[1],
        device_id={"region": fast_peer}, device_id_type=MESH,
    )

    load_wait(0)
    mix(0)
    (start_norm,) = scalar_finish(0, 1)
    rescale = sectors * width / start_norm

    def store_slow(v, value):
        for k in range(slabs):
            out_slow[k, v] = value[k * rows : (k + 1) * rows]

    carry_env(0, rescale, store_slow)

    @pl.when(inner)
    def _():
        for k in range(slabs - AHEAD):
            slow_copy(k).start()

    load_wait(1)
    mix(1)

    def store_fast(v, value):
        out_fast[v] = value

    carry_env(1, rescale, store_fast)
    fast_copy.start()

    @pl.when(jnp.logical_and(edge, even))
    def _():
        def body(v, carry):
            for k in range(slabs):
                slow[k, v] = env[1, v, k * rows : (k + 1) * rows, :]
            return carry

        lax.fori_loop(0, terms, body, 0)

    @pl.when(jnp.logical_and(edge, jnp.logical_not(even)))
    def _():
        def body(v, carry):
            value = nt(unit[...], env[1, v]).astype(BF16)
            for k in range(slabs):
                slow[k, v] = value[k * rows : (k + 1) * rows]
            return carry

        lax.fori_loop(0, terms, body, 0)

    vec[0] = (frame[0].astype(F32) * jnp.sqrt(cells / start_norm)).astype(BF16)
    diag = diag_ref[...]
    diag_frame = jnp.where(even, diag, nt(unit[...], diag).astype(BF16))
    inv_root = 1.0 / math.sqrt(terms)

    def y_copy(it, k, d):
        peer_y = lax.rem(my_y + d, ys)
        return pltpu.make_async_remote_copy(
            src_ref=part[it].at[k, peer_y], dst_ref=y_in[it].at[k, d - 1],
            send_sem=y_send.at[it, k, d - 1], recv_sem=y_recv.at[it, k, d - 1],
            device_id={"sector": my_z * ys + peer_y}, device_id_type=MESH,
        )

    def z_copy(it, k, d):
        peer_z = lax.rem(my_z + d, zs)
        return pltpu.make_async_remote_copy(
            src_ref=zsum[it].at[k, peer_z], dst_ref=z_in[it].at[k, d - 1],
            send_sem=z_send.at[it, k, d - 1], recv_sem=z_recv.at[it, k, d - 1],
            device_id={"sector": peer_z * ys + my_y}, device_id_type=MESH,
        )

    def z_phase(it, k):
        for d in range(1, ys):
            y_copy(it, k, d).wait_recv()
        added = part[it][k, my_y].astype(F32)
        for d in range(1, ys):
            added = added + y_in[it][k, d - 1].astype(F32)
        zsum[it][k] = added.astype(BF16)
        for d in range(1, zs):
            z_copy(it, k, d).start()

    def apply(it):
        merge = slabs // SLABS[it]
        tile = merge * rows

        def z_before(k):
            @pl.when(k >= 1)
            def _():
                z_phase(it, k - 1)

        def body(k, carry):
            if it == 0:
                z_before(k)

                @pl.when(inner)
                def _():
                    slow_copy(k).wait_recv()

                @pl.when(jnp.logical_and(inner, k < AHEAD))
                def _():
                    slow_copy(k).wait_send()
                    slow_copy(k + slabs - AHEAD).start()

            left = slow[pl.ds(k * merge, merge)].reshape(merge * terms * rows, width)
            half = nn(left, vec[it]).astype(BF16)
            for w in range(terms):
                pieces = [
                    half[(j * terms + w) * rows : (j * terms + w + 1) * rows] for j in range(merge)
                ]
                term[w, 0:tile, :] = nn(jnp.concatenate(pieces, axis=0), fast[w])
            matrix = route[...]
            for i in range(tile // 16):
                halves = []
                for h in range(2):
                    at = 16 * i + 8 * h
                    piece = term[:, at : at + 8, :].reshape(tall, width).astype(BF16)
                    halves.append((nn(matrix, piece) * inv_root).reshape(ys, zs, 8, width))
                both = jnp.concatenate(halves, axis=2).astype(BF16)
                part[it][k, :, :, 16 * i : 16 * i + 16, :] = both
            for d in range(1, ys):
                y_copy(it, k, d).start()
            if it > 0:
                z_before(k)
            return carry

        lax.fori_loop(0, SLABS[it], body, 0)
        z_phase(it, SLABS[it] - 1)
        for k in range(SLABS[it]):
            for d in range(1, zs):
                z_copy(it, k, d).wait_recv()
            added = zsum[it][k, my_z].astype(F32)
            for d in range(1, zs):
                added = added + z_in[it][k, d - 1].astype(F32)
            result[it, k * tile : (k + 1) * tile, :] = added
        source = vec[it].astype(F32)
        value = jnp.where(keep, result[it] + diag_frame.astype(F32) * source, 0.0)
        result[it] = value

    fast_copy.wait_recv()
    apply(0)
    first = result[0]
    vec[1] = first.astype(BF16)
    start = vec[0].astype(F32)
    scalar_start(1, [total(start * start), total(start * first), total(first * first)])
    apply(1)
    vv, vh, hh = scalar_finish(1, 3)
    energy = vh / vv
    near = 1.0 + STEP * energy
    scale = jnp.sqrt(cells / jnp.maximum(near * near * vv - 2.0 * STEP * near * vh + STEP * STEP * hh, vv))
    start = vec[0].astype(F32)
    first = result[0]
    x = scale * near * start - scale * STEP * first
    applied = scale * near * first - scale * STEP * result[1]
    y = applied - energy * x
    result[0] = x
    result[1] = y
    scalar_start(2, [total(x * x), total(x * y), total(y * y)])
    xx, xy, yy = scalar_finish(2, 3)
    gap = xy / xx
    norm = xx + STEP * STEP * jnp.maximum(yy - gap * xy, 0.0)
    grow = jnp.sqrt(cells / norm)
    bond = (grow * (result[0] - STEP * (result[1] - gap * result[0]))).astype(BF16)

    @pl.when(even)
    def _():
        bond_ref[...] = bond

    @pl.when(jnp.logical_not(even))
    def _():
        bond_ref[...] = nt(unit[...], bond).astype(BF16)

    energy_ref[...] = jnp.broadcast_to(energy + gap, (1, 128))

    for which in range(3):
        for d in range(1, sectors):
            scalar_copy(which, d).wait_send()
    fast_copy.wait_send()

    @pl.when(inner)
    def _():
        for k in range(AHEAD, slabs):
            slow_copy(k).wait_send()

    for it in range(ITERS):
        for k in range(SLABS[it]):
            for d in range(1, ys):
                y_copy(it, k, d).wait_send()
            for d in range(1, zs):
                z_copy(it, k, d).wait_send()


def local(regions, ys, zs, psi, left_env, right_env, diagonal, lc, rc, mask, target, size):
    width, terms = psi.shape[-1], left_env.shape[2]
    sectors, slabs = ys * zs, SLABS[0]
    rows, tiles = width // slabs, [width // n for n in SLABS]
    y_peers, z_peers = max(ys - 1, 1), max(zs - 1, 1)
    envs = (terms, width, width)
    vmem = pl.BlockSpec(memory_space=pltpu.VMEM)
    smem = pl.BlockSpec(memory_space=pltpu.SMEM)
    hbm = pl.BlockSpec(memory_space=pl.ANY)
    dma = pltpu.SemaphoreType.DMA
    bond, energy = pl.pallas_call(
        functools.partial(kernel, regions, ys, zs, width, terms),
        out_shape=(
            jax.ShapeDtypeStruct((width, width), BF16),
            jax.ShapeDtypeStruct((1, 128), F32),
        ),
        in_specs=[vmem, hbm, hbm, vmem, vmem, vmem, vmem, smem, smem],
        out_specs=(vmem, vmem),
        scratch_shapes=[
            pltpu.VMEM((2,) + envs, BF16),
            pltpu.VMEM(envs, BF16),
            pltpu.VMEM((2, width, width), BF16),
            pltpu.VMEM((slabs, terms, rows, width), BF16),
            pltpu.VMEM(envs, BF16),
            pltpu.VMEM((slabs, terms, rows, width), BF16),
            pltpu.VMEM(envs, BF16),
            pltpu.VMEM((2, width, width), BF16),
            pltpu.VMEM((width, width), BF16),
            pltpu.VMEM((sectors * 8, terms * 8), BF16),
            pltpu.VMEM((terms, max(tiles), width), F32),
            *[pltpu.VMEM((n, ys, zs, width // n, width), BF16) for n in SLABS],
            *[pltpu.VMEM((n, y_peers, zs, width // n, width), BF16) for n in SLABS],
            *[pltpu.VMEM((n, zs, width // n, width), BF16) for n in SLABS],
            *[pltpu.VMEM((n, z_peers, width // n, width), BF16) for n in SLABS],
            pltpu.VMEM((2, width, width), F32),
            pltpu.VMEM((3, sectors, 8, 128), F32),
            dma((2,)),
            dma((slabs,)),
            dma((slabs,)),
            dma((2,)),
            dma((ITERS, slabs, y_peers)),
            dma((ITERS, slabs, y_peers)),
            dma((ITERS, slabs, z_peers)),
            dma((ITERS, slabs, z_peers)),
            dma((3, sectors - 1)),
            dma((3, sectors - 1)),
        ],
        compiler_params=pltpu.CompilerParams(
            collective_id=0, has_side_effects=True, vmem_limit_bytes=56 * 2**20
        ),
    )(
        psi.reshape(width, width), left_env.reshape(envs), right_env.reshape(envs),
        diagonal.reshape(width, width), lc, rc, mask, target, size,
    )
    return bond.reshape(1, 1, width, width), energy[0, :1]


def solution(mesh):
    regions, sectors = mesh.shape["region"], mesh.shape["sector"]
    ys = 1
    while (2 * ys) * (2 * ys) * 2 <= sectors:
        ys *= 2
    in_specs = (
        P("region", "sector", None, None),
        P("region", "sector", None, None, None),
        P("region", "sector", None, None, None),
        P("region", "sector", None, None),
        P(),
        P(),
        P(),
        P("sector", None),
        P("sector"),
    )
    out_specs = (P("region", "sector", None, None), P("region"))
    body = functools.partial(local, regions, ys, sectors // ys)
    return jax.shard_map(body, mesh=mesh, in_specs=in_specs, out_specs=out_specs, check_vma=False)
```

```python
import functools
import math

import jax
import jax.numpy as jnp
from jax import lax
from jax.experimental import pallas as pl
from jax.experimental.pallas import tpu as pltpu
from jax.sharding import PartitionSpec as P

ITERS = 2
STEP = 0.5
SLABS = (4, 4)
LAGS = (1, 2)
AHEAD = 1
F32 = jnp.float32
BF16 = jnp.bfloat16
MESH = pl.DeviceIdType.MESH


def nn(a, b):
    return lax.dot_general(a, b, (((1,), (0,)), ((), ())), preferred_element_type=F32)


def nt(a, b):
    return lax.dot_general(a, b, (((1,), (1,)), ((), ())), preferred_element_type=F32)


def iota(shape, dim):
    return lax.broadcasted_iota(jnp.int32, shape, dim)


def total(x):
    return jnp.sum(jnp.sum(x, axis=0, keepdims=True), axis=1, keepdims=True)


def kernel(
    regions, ys, zs, width, terms,
    psi_ref, left_hbm, right_hbm, diag_ref, lc_ref, rc_ref, mask_ref, target_ref, size_ref,
    bond_ref, energy_ref,
    env, mixed, frame, out_slow, out_fast, slow, fast, vec, unit, route,
    term, part0, part1, y_in0, y_in1, zsum0, zsum1, z_in0, z_in1, result, scal,
    load_sem, slow_send, slow_recv, fast_sem, y_send, y_recv, z_send, z_recv, s_send, s_recv,
):
    sectors = ys * zs
    part, y_in = (part0, part1), (y_in0, y_in1)
    zsum, z_in = (zsum0, zsum1), (z_in0, z_in1)
    slabs = SLABS[0]
    rows = width // slabs
    cells = float(sectors * width * width)
    region = lax.axis_index("region")
    me = lax.axis_index("sector")
    my_y, my_z = lax.rem(me, ys), lax.div(me, ys)
    odd = lax.rem(region, 2)
    even = odd == 0
    fast_peer = region + 1 - 2 * odd
    slow_peer = region - 1 + 2 * odd
    inner = jnp.logical_and(slow_peer >= 0, slow_peer < regions)
    edge = jnp.logical_not(inner)

    barrier = pltpu.get_barrier_semaphore()
    for d in range(1, sectors):
        pl.semaphore_signal(
            barrier, inc=1, device_id={"sector": lax.rem(me + d, sectors)}, device_id_type=MESH
        )
    pl.semaphore_signal(barrier, inc=1, device_id={"region": fast_peer}, device_id_type=MESH)

    @pl.when(inner)
    def _():
        pl.semaphore_signal(barrier, inc=1, device_id={"region": slow_peer}, device_id_type=MESH)

    def load(source, slot):
        return pltpu.make_async_copy(source, env.at[slot], load_sem.at[slot])

    @pl.when(even)
    def _():
        load(right_hbm, 0).start()
        load(left_hbm, 1).start()

    @pl.when(jnp.logical_not(even))
    def _():
        load(left_hbm, 0).start()
        load(right_hbm, 1).start()

    size = size_ref[0]
    square = (width, width)
    keep = jnp.logical_and(iota(square, 0) < size, iota(square, 1) < size)
    unit[...] = jnp.where(iota(square, 0) == iota(square, 1), 1.0, 0.0).astype(BF16)
    wide = jnp.where(keep, psi_ref[...].astype(F32), 0.0)
    masked = wide.astype(BF16)
    turned = nt(unit[...], masked).astype(BF16)

    @pl.when(even)
    def _():
        frame[0] = masked
        frame[1] = turned

    @pl.when(jnp.logical_not(even))
    def _():
        frame[0] = turned
        frame[1] = masked

    lanes = iota((8, 128), 1)

    def scalar_copy(which, d):
        peer = lax.rem(me + d, sectors)
        return pltpu.make_async_remote_copy(
            src_ref=scal.at[which, me], dst_ref=scal.at[which, me],
            send_sem=s_send.at[which, d - 1], recv_sem=s_recv.at[which, d - 1],
            device_id={"sector": peer}, device_id_type=MESH,
        )

    def scalar_start(which, values):
        packed = jnp.zeros((8, 128), F32)
        for lane, value in enumerate(values):
            packed = jnp.where(lanes == lane, jnp.broadcast_to(value, (8, 128)), packed)
        scal[which, me] = packed
        for d in range(1, sectors):
            scalar_copy(which, d).start()

    def scalar_finish(which, count):
        for d in range(1, sectors):
            scalar_copy(which, d).wait_recv()
        added = jnp.sum(scal[which], axis=0)[0:1, :]
        return [
            jnp.sum(jnp.where(lanes[0:1] == lane, added, 0.0), axis=1, keepdims=True)
            for lane in range(count)
        ]

    pl.semaphore_wait(barrier, sectors + inner.astype(jnp.int32))

    scalar_start(0, [total(wide * wide)])

    tall = 8 * terms
    spread = jnp.where((iota((tall, terms), 0) >> 3) == iota((tall, terms), 1), 1.0, 0.0).astype(BF16)
    same = (iota((tall, tall), 0) & 7) == (iota((tall, tall), 1) & 7)
    pattern = mask_ref[...].astype(F32)

    def mixer(coeff):
        over = nn(spread, (coeff * pattern).astype(BF16)).astype(BF16)
        return jnp.where(same, nt(over, spread), 0.0).astype(BF16)

    left_c, right_c = lc_ref[...], rc_ref[...]
    parity = odd.astype(F32)
    mixers = [
        mixer(right_c + parity * (left_c - right_c)),
        mixer(left_c + parity * (right_c - left_c)),
    ]
    wanted = (sectors * 8, tall)
    aim = jnp.zeros(wanted, jnp.int32)
    for w in range(terms):
        aim = jnp.where((iota(wanted, 1) >> 3) == w, target_ref[0, w], aim)
    block = iota(wanted, 0) >> 3
    z_bits = zs.bit_length() - 1
    mine = (block & (zs - 1)) * ys + (block >> z_bits)
    hit = jnp.logical_and(aim == mine, (iota(wanted, 0) & 7) == (iota(wanted, 1) & 7))
    route[...] = jnp.where(hit, 1.0, 0.0).astype(BF16)

    def mix(slot):
        matrix = mixers[slot]

        def body(i, carry):
            for j in range(4):
                start = pl.multiple_of(i * 64 + j * 16, 16)
                x = env[slot, :, pl.ds(start, 16), :].astype(F32)
                halves = []
                for h in range(2):
                    piece = x[:, 8 * h : 8 * h + 8, :].reshape(tall, width).astype(BF16)
                    halves.append(nn(matrix, piece).reshape(terms, 8, width))
                mixed[:, pl.ds(start, 16), :] = jnp.concatenate(halves, axis=1).astype(BF16)
            return carry

        lax.fori_loop(0, width // 64, body, 0)

    group = max(g for g in range(1, 10) if terms % g == 0)

    def carry_env(slot, rescale, store):
        def body(i, carry):
            for j in range(group):
                v = i * group + j
                a = frame[slot]
                y = nn(a, mixed[v]).astype(BF16)
                first = jnp.where(even, a, y)
                second = jnp.where(even, y, a)
                store(v, (rescale * nt(first, second)).astype(BF16))
            return carry

        lax.fori_loop(0, terms // group, body, 0)

    def load_wait(slot):
        load(left_hbm, slot).wait()

    def slow_copy(k):
        return pltpu.make_async_remote_copy(
            src_ref=out_slow.at[k], dst_ref=slow.at[k],
            send_sem=slow_send.at[k], recv_sem=slow_recv.at[k],
            device_id={"region": slow_peer}, device_id_type=MESH,
        )

    fast_copy = pltpu.make_async_remote_copy(
        src_ref=out_fast, dst_ref=fast, send_sem=fast_sem.at[0], recv_sem=fast_sem.at[1],
        device_id={"region": fast_peer}, device_id_type=MESH,
    )

    load_wait(0)
    mix(0)
    (start_norm,) = scalar_finish(0, 1)
    rescale = sectors * width / start_norm

    def store_slow(v, value):
        for k in range(slabs):
            out_slow[k, v] = value[k * rows : (k + 1) * rows]

    carry_env(0, rescale, store_slow)

    @pl.when(inner)
    def _():
        for k in range(AHEAD):
            slow_copy(k).start()

    load_wait(1)
    mix(1)

    def store_fast(v, value):
        out_fast[v] = value

    carry_env(1, rescale, store_fast)
    fast_copy.start()

    @pl.when(inner)
    def _():
        for k in range(AHEAD, slabs):
            slow_copy(k).start()

    @pl.when(jnp.logical_and(edge, even))
    def _():
        def body(v, carry):
            for k in range(slabs):
                slow[k, v] = env[1, v, k * rows : (k + 1) * rows, :]
            return carry

        lax.fori_loop(0, terms, body, 0)

    @pl.when(jnp.logical_and(edge, jnp.logical_not(even)))
    def _():
        def body(v, carry):
            value = nt(unit[...], env[1, v]).astype(BF16)
            for k in range(slabs):
                slow[k, v] = value[k * rows : (k + 1) * rows]
            return carry

        lax.fori_loop(0, terms, body, 0)

    vec[0] = (frame[0].astype(F32) * jnp.sqrt(cells / start_norm)).astype(BF16)
    diag = diag_ref[...]
    diag_frame = jnp.where(even, diag, nt(unit[...], diag).astype(BF16))
    inv_root = 1.0 / math.sqrt(terms)

    def y_copy(it, k, d):
        peer_y = lax.rem(my_y + d, ys)
        return pltpu.make_async_remote_copy(
            src_ref=part[it].at[k, peer_y], dst_ref=y_in[it].at[k, d - 1],
            send_sem=y_send.at[it, k, d - 1], recv_sem=y_recv.at[it, k, d - 1],
            device_id={"sector": my_z * ys + peer_y}, device_id_type=MESH,
        )

    def z_copy(it, k, d):
        peer_z = lax.rem(my_z + d, zs)
        return pltpu.make_async_remote_copy(
            src_ref=zsum[it].at[k, peer_z], dst_ref=z_in[it].at[k, d - 1],
            send_sem=z_send.at[it, k, d - 1], recv_sem=z_recv.at[it, k, d - 1],
            device_id={"sector": peer_z * ys + my_y}, device_id_type=MESH,
        )

    def z_phase(it, k):
        for d in range(1, ys):
            y_copy(it, k, d).wait_recv()
        added = part[it][k, my_y].astype(F32)
        for d in range(1, ys):
            added = added + y_in[it][k, d - 1].astype(F32)
        zsum[it][k] = added.astype(BF16)
        for d in range(1, zs):
            z_copy(it, k, d).start()

    def apply(it):
        merge = slabs // SLABS[it]
        tile = merge * rows

        lag = LAGS[it]

        def body(k, carry):
            if it == 0:
                @pl.when(inner)
                def _():
                    slow_copy(k).wait_recv()

            left = slow[pl.ds(k * merge, merge)].reshape(merge * terms * rows, width)
            half = nn(left, vec[it]).astype(BF16)
            for w in range(terms):
                pieces = [
                    half[(j * terms + w) * rows : (j * terms + w + 1) * rows] for j in range(merge)
                ]
                term[w, 0:tile, :] = nn(jnp.concatenate(pieces, axis=0), fast[w])
            matrix = route[...]
            for i in range(tile // 16):
                halves = []
                for h in range(2):
                    at = 16 * i + 8 * h
                    piece = term[:, at : at + 8, :].reshape(tall, width).astype(BF16)
                    halves.append((nn(matrix, piece) * inv_root).reshape(ys, zs, 8, width))
                both = jnp.concatenate(halves, axis=2).astype(BF16)
                part[it][k, :, :, 16 * i : 16 * i + 16, :] = both
            for d in range(1, ys):
                y_copy(it, k, d).start()

            @pl.when(k >= lag)
            def _():
                z_phase(it, k - lag)

            return carry

        lax.fori_loop(0, SLABS[it], body, 0)
        for k in range(SLABS[it] - lag, SLABS[it]):
            z_phase(it, k)
        for k in range(SLABS[it]):
            for d in range(1, zs):
                z_copy(it, k, d).wait_recv()
            added = zsum[it][k, my_z].astype(F32)
            for d in range(1, zs):
                added = added + z_in[it][k, d - 1].astype(F32)
            result[it, k * tile : (k + 1) * tile, :] = added
        source = vec[it].astype(F32)
        value = jnp.where(keep, result[it] + diag_frame.astype(F32) * source, 0.0)
        result[it] = value

    fast_copy.wait_recv()
    apply(0)
    first = result[0]
    vec[1] = first.astype(BF16)
    start = vec[0].astype(F32)
    scalar_start(1, [total(start * start), total(start * first), total(first * first)])
    apply(1)
    vv, vh, hh = scalar_finish(1, 3)
    energy = vh / vv
    near = 1.0 + STEP * energy
    scale = jnp.sqrt(cells / jnp.maximum(near * near * vv - 2.0 * STEP * near * vh + STEP * STEP * hh, vv))
    start = vec[0].astype(F32)
    first = result[0]
    x = scale * near * start - scale * STEP * first
    applied = scale * near * first - scale * STEP * result[1]
    y = applied - energy * x
    result[0] = x
    result[1] = y
    scalar_start(2, [total(x * x), total(x * y), total(y * y)])
    xx, xy, yy = scalar_finish(2, 3)
    gap = xy / xx
    norm = xx + STEP * STEP * jnp.maximum(yy - gap * xy, 0.0)
    grow = jnp.sqrt(cells / norm)
    bond = (grow * (result[0] - STEP * (result[1] - gap * result[0]))).astype(BF16)

    @pl.when(even)
    def _():
        bond_ref[...] = bond

    @pl.when(jnp.logical_not(even))
    def _():
        bond_ref[...] = nt(unit[...], bond).astype(BF16)

    energy_ref[...] = jnp.broadcast_to(energy + gap, (1, 128))

    for which in range(3):
        for d in range(1, sectors):
            scalar_copy(which, d).wait_send()
    fast_copy.wait_send()

    @pl.when(inner)
    def _():
        for k in range(slabs):
            slow_copy(k).wait_send()

    for it in range(ITERS):
        for k in range(SLABS[it]):
            for d in range(1, ys):
                y_copy(it, k, d).wait_send()
            for d in range(1, zs):
                z_copy(it, k, d).wait_send()


def local(regions, ys, zs, psi, left_env, right_env, diagonal, lc, rc, mask, target, size):
    width, terms = psi.shape[-1], left_env.shape[2]
    sectors, slabs = ys * zs, SLABS[0]
    rows, tiles = width // slabs, [width // n for n in SLABS]
    y_peers, z_peers = max(ys - 1, 1), max(zs - 1, 1)
    envs = (terms, width, width)
    vmem = pl.BlockSpec(memory_space=pltpu.VMEM)
    smem = pl.BlockSpec(memory_space=pltpu.SMEM)
    hbm = pl.BlockSpec(memory_space=pl.ANY)
    dma = pltpu.SemaphoreType.DMA
    bond, energy = pl.pallas_call(
        functools.partial(kernel, regions, ys, zs, width, terms),
        out_shape=(
            jax.ShapeDtypeStruct((width, width), BF16),
            jax.ShapeDtypeStruct((1, 128), F32),
        ),
        in_specs=[vmem, hbm, hbm, vmem, vmem, vmem, vmem, smem, smem],
        out_specs=(vmem, vmem),
        scratch_shapes=[
            pltpu.VMEM((2,) + envs, BF16),
            pltpu.VMEM(envs, BF16),
            pltpu.VMEM((2, width, width), BF16),
            pltpu.VMEM((slabs, terms, rows, width), BF16),
            pltpu.VMEM(envs, BF16),
            pltpu.VMEM((slabs, terms, rows, width), BF16),
            pltpu.VMEM(envs, BF16),
            pltpu.VMEM((2, width, width), BF16),
            pltpu.VMEM((width, width), BF16),
            pltpu.VMEM((sectors * 8, terms * 8), BF16),
            pltpu.VMEM((terms, max(tiles), width), F32),
            *[pltpu.VMEM((n, ys, zs, width // n, width), BF16) for n in SLABS],
            *[pltpu.VMEM((n, y_peers, zs, width // n, width), BF16) for n in SLABS],
            *[pltpu.VMEM((n, zs, width // n, width), BF16) for n in SLABS],
            *[pltpu.VMEM((n, z_peers, width // n, width), BF16) for n in SLABS],
            pltpu.VMEM((2, width, width), F32),
            pltpu.VMEM((3, sectors, 8, 128), F32),
            dma((2,)),
            dma((slabs,)),
            dma((slabs,)),
            dma((2,)),
            dma((ITERS, slabs, y_peers)),
            dma((ITERS, slabs, y_peers)),
            dma((ITERS, slabs, z_peers)),
            dma((ITERS, slabs, z_peers)),
            dma((3, sectors - 1)),
            dma((3, sectors - 1)),
        ],
        compiler_params=pltpu.CompilerParams(
            collective_id=0, has_side_effects=True, vmem_limit_bytes=56 * 2**20
        ),
    )(
        psi.reshape(width, width), left_env.reshape(envs), right_env.reshape(envs),
        diagonal.reshape(width, width), lc, rc, mask, target, size,
    )
    return bond.reshape(1, 1, width, width), energy[0, :1]


def solution(mesh):
    regions, sectors = mesh.shape["region"], mesh.shape["sector"]
    ys = 1
    while (2 * ys) * (2 * ys) * 2 <= sectors:
        ys *= 2
    in_specs = (
        P("region", "sector", None, None),
        P("region", "sector", None, None, None),
        P("region", "sector", None, None, None),
        P("region", "sector", None, None),
        P(),
        P(),
        P(),
        P("sector", None),
        P("sector"),
    )
    out_specs = (P("region", "sector", None, None), P("region"))
    body = functools.partial(local, regions, ys, sectors // ys)
    return jax.shard_map(body, mesh=mesh, in_specs=in_specs, out_specs=out_specs, check_vma=False)
```

```python
import functools
import math

import jax
import jax.numpy as jnp
from jax import lax
from jax.experimental import pallas as pl
from jax.experimental.pallas import tpu as pltpu
from jax.sharding import PartitionSpec as P

ITERS = 2
STEP = 0.5
SLABS = (4, 4)
LAGS = (1, 2)
AHEAD = 1
F32 = jnp.float32
BF16 = jnp.bfloat16
MESH = pl.DeviceIdType.MESH


def nn(a, b):
    return lax.dot_general(a, b, (((1,), (0,)), ((), ())), preferred_element_type=F32)


def nt(a, b):
    return lax.dot_general(a, b, (((1,), (1,)), ((), ())), preferred_element_type=F32)


def iota(shape, dim):
    return lax.broadcasted_iota(jnp.int32, shape, dim)


def total(x):
    return jnp.sum(jnp.sum(x, axis=0, keepdims=True), axis=1, keepdims=True)


def kernel(
    regions, ys, zs, width, terms,
    psi_ref, left_hbm, right_hbm, diag_ref, lc_ref, rc_ref, mask_ref, target_ref, size_ref,
    bond_ref, energy_ref, hbm_out, hbm_in,
    env, mixed, frame, out_slow, out_fast, slow, fast, vec, unit, route,
    term, part0, part1, y_in0, y_in1, zsum0, zsum1, z_in0, z_in1, result, scal,
    load_sem, stage_sem, slow_send, slow_recv, fast_sem, y_send, y_recv, z_send, z_recv, s_send, s_recv,
):
    sectors = ys * zs
    part, y_in = (part0, part1), (y_in0, y_in1)
    zsum, z_in = (zsum0, zsum1), (z_in0, z_in1)
    slabs = SLABS[0]
    rows = width // slabs
    cells = float(sectors * width * width)
    region = lax.axis_index("region")
    me = lax.axis_index("sector")
    my_y, my_z = lax.rem(me, ys), lax.div(me, ys)
    odd = lax.rem(region, 2)
    even = odd == 0
    fast_peer = region + 1 - 2 * odd
    slow_peer = region - 1 + 2 * odd
    inner = jnp.logical_and(slow_peer >= 0, slow_peer < regions)
    edge = jnp.logical_not(inner)

    barrier = pltpu.get_barrier_semaphore()
    for d in range(1, sectors):
        pl.semaphore_signal(
            barrier, inc=1, device_id={"sector": lax.rem(me + d, sectors)}, device_id_type=MESH
        )
    pl.semaphore_signal(barrier, inc=1, device_id={"region": fast_peer}, device_id_type=MESH)

    @pl.when(inner)
    def _():
        pl.semaphore_signal(barrier, inc=1, device_id={"region": slow_peer}, device_id_type=MESH)

    def load(source, slot):
        return pltpu.make_async_copy(source, env.at[slot], load_sem.at[slot])

    @pl.when(even)
    def _():
        load(right_hbm, 0).start()
        load(left_hbm, 1).start()

    @pl.when(jnp.logical_not(even))
    def _():
        load(left_hbm, 0).start()
        load(right_hbm, 1).start()

    size = size_ref[0]
    square = (width, width)
    keep = jnp.logical_and(iota(square, 0) < size, iota(square, 1) < size)
    unit[...] = jnp.where(iota(square, 0) == iota(square, 1), 1.0, 0.0).astype(BF16)
    wide = jnp.where(keep, psi_ref[...].astype(F32), 0.0)
    masked = wide.astype(BF16)
    turned = nt(unit[...], masked).astype(BF16)

    @pl.when(even)
    def _():
        frame[0] = masked
        frame[1] = turned

    @pl.when(jnp.logical_not(even))
    def _():
        frame[0] = turned
        frame[1] = masked

    lanes = iota((8, 128), 1)

    def scalar_copy(which, d):
        peer = lax.rem(me + d, sectors)
        return pltpu.make_async_remote_copy(
            src_ref=scal.at[which, me], dst_ref=scal.at[which, me],
            send_sem=s_send.at[which, d - 1], recv_sem=s_recv.at[which, d - 1],
            device_id={"sector": peer}, device_id_type=MESH,
        )

    def scalar_start(which, values):
        packed = jnp.zeros((8, 128), F32)
        for lane, value in enumerate(values):
            packed = jnp.where(lanes == lane, jnp.broadcast_to(value, (8, 128)), packed)
        scal[which, me] = packed
        for d in range(1, sectors):
            scalar_copy(which, d).start()

    def scalar_finish(which, count):
        for d in range(1, sectors):
            scalar_copy(which, d).wait_recv()
        added = jnp.sum(scal[which], axis=0)[0:1, :]
        return [
            jnp.sum(jnp.where(lanes[0:1] == lane, added, 0.0), axis=1, keepdims=True)
            for lane in range(count)
        ]

    pl.semaphore_wait(barrier, sectors + inner.astype(jnp.int32))

    scalar_start(0, [total(wide * wide)])

    tall = 8 * terms
    spread = jnp.where((iota((tall, terms), 0) >> 3) == iota((tall, terms), 1), 1.0, 0.0).astype(BF16)
    same = (iota((tall, tall), 0) & 7) == (iota((tall, tall), 1) & 7)
    pattern = mask_ref[...].astype(F32)

    def mixer(coeff):
        over = nn(spread, (coeff * pattern).astype(BF16)).astype(BF16)
        return jnp.where(same, nt(over, spread), 0.0).astype(BF16)

    left_c, right_c = lc_ref[...], rc_ref[...]
    parity = odd.astype(F32)
    mixers = [
        mixer(right_c + parity * (left_c - right_c)),
        mixer(left_c + parity * (right_c - left_c)),
    ]
    wanted = (sectors * 8, tall)
    aim = jnp.zeros(wanted, jnp.int32)
    for w in range(terms):
        aim = jnp.where((iota(wanted, 1) >> 3) == w, target_ref[0, w], aim)
    block = iota(wanted, 0) >> 3
    z_bits = zs.bit_length() - 1
    mine = (block & (zs - 1)) * ys + (block >> z_bits)
    hit = jnp.logical_and(aim == mine, (iota(wanted, 0) & 7) == (iota(wanted, 1) & 7))
    route[...] = jnp.where(hit, 1.0, 0.0).astype(BF16)

    def mix(slot):
        matrix = mixers[slot]

        def body(i, carry):
            for j in range(4):
                start = pl.multiple_of(i * 64 + j * 16, 16)
                x = env[slot, :, pl.ds(start, 16), :].astype(F32)
                halves = []
                for h in range(2):
                    piece = x[:, 8 * h : 8 * h + 8, :].reshape(tall, width).astype(BF16)
                    halves.append(nn(matrix, piece).reshape(terms, 8, width))
                mixed[:, pl.ds(start, 16), :] = jnp.concatenate(halves, axis=1).astype(BF16)
            return carry

        lax.fori_loop(0, width // 64, body, 0)

    group = max(g for g in range(1, 10) if terms % g == 0)

    def carry_env(slot, rescale, store):
        def body(i, carry):
            for j in range(group):
                v = i * group + j
                a = frame[slot]
                y = nn(a, mixed[v]).astype(BF16)
                first = jnp.where(even, a, y)
                second = jnp.where(even, y, a)
                store(v, (rescale * nt(first, second)).astype(BF16))
            return carry

        lax.fori_loop(0, terms // group, body, 0)

    def load_wait(slot):
        load(left_hbm, slot).wait()

    def slow_copy(k):
        return pltpu.make_async_remote_copy(
            src_ref=hbm_out.at[k], dst_ref=hbm_in.at[k],
            send_sem=slow_send.at[k], recv_sem=slow_recv.at[k],
            device_id={"region": slow_peer}, device_id_type=MESH,
        )

    def stage_out(k):
        return pltpu.make_async_copy(out_slow.at[k], hbm_out.at[k], stage_sem.at[0, k])

    def stage_in(k):
        return pltpu.make_async_copy(hbm_in.at[k], slow.at[k], stage_sem.at[1, k])

    fast_copy = pltpu.make_async_remote_copy(
        src_ref=out_fast, dst_ref=fast, send_sem=fast_sem.at[0], recv_sem=fast_sem.at[1],
        device_id={"region": fast_peer}, device_id_type=MESH,
    )

    load_wait(0)
    mix(0)
    (start_norm,) = scalar_finish(0, 1)
    rescale = sectors * width / start_norm

    def store_slow(v, value):
        for k in range(slabs):
            out_slow[k, v] = value[k * rows : (k + 1) * rows]

    carry_env(0, rescale, store_slow)

    @pl.when(inner)
    def _():
        for k in range(slabs):
            stage_out(k).start()
        for k in range(AHEAD):
            stage_out(k).wait()
            slow_copy(k).start()

    load_wait(1)
    mix(1)

    def store_fast(v, value):
        out_fast[v] = value

    carry_env(1, rescale, store_fast)
    fast_copy.start()

    @pl.when(inner)
    def _():
        for k in range(AHEAD, slabs):
            stage_out(k).wait()
            slow_copy(k).start()

    @pl.when(jnp.logical_and(edge, even))
    def _():
        def body(v, carry):
            for k in range(slabs):
                slow[k, v] = env[1, v, k * rows : (k + 1) * rows, :]
            return carry

        lax.fori_loop(0, terms, body, 0)

    @pl.when(jnp.logical_and(edge, jnp.logical_not(even)))
    def _():
        def body(v, carry):
            value = nt(unit[...], env[1, v]).astype(BF16)
            for k in range(slabs):
                slow[k, v] = value[k * rows : (k + 1) * rows]
            return carry

        lax.fori_loop(0, terms, body, 0)

    vec[0] = (frame[0].astype(F32) * jnp.sqrt(cells / start_norm)).astype(BF16)
    diag = diag_ref[...]
    diag_frame = jnp.where(even, diag, nt(unit[...], diag).astype(BF16))
    inv_root = 1.0 / math.sqrt(terms)

    def y_copy(it, k, d):
        peer_y = lax.rem(my_y + d, ys)
        return pltpu.make_async_remote_copy(
            src_ref=part[it].at[k, peer_y], dst_ref=y_in[it].at[k, d - 1],
            send_sem=y_send.at[it, k, d - 1], recv_sem=y_recv.at[it, k, d - 1],
            device_id={"sector": my_z * ys + peer_y}, device_id_type=MESH,
        )

    def z_copy(it, k, d):
        peer_z = lax.rem(my_z + d, zs)
        return pltpu.make_async_remote_copy(
            src_ref=zsum[it].at[k, peer_z], dst_ref=z_in[it].at[k, d - 1],
            send_sem=z_send.at[it, k, d - 1], recv_sem=z_recv.at[it, k, d - 1],
            device_id={"sector": peer_z * ys + my_y}, device_id_type=MESH,
        )

    def z_phase(it, k):
        for d in range(1, ys):
            y_copy(it, k, d).wait_recv()
        added = part[it][k, my_y].astype(F32)
        for d in range(1, ys):
            added = added + y_in[it][k, d - 1].astype(F32)
        zsum[it][k] = added.astype(BF16)
        for d in range(1, zs):
            z_copy(it, k, d).start()

    def apply(it):
        merge = slabs // SLABS[it]
        tile = merge * rows

        lag = LAGS[it]

        def body(k, carry):
            if it == 0:
                @pl.when(inner)
                def _():
                    slow_copy(k).wait_recv()
                    stage_in(k).start()
                    stage_in(k).wait()

            if it == 0:
                half = nn(slow[k].reshape(terms * rows, width), vec[it]).astype(BF16)
                for w in range(terms):
                    term[w, 0:rows, :] = nn(half[w * rows : (w + 1) * rows], fast[w])
                base = 0
            else:
                base = pl.multiple_of(k * tile, tile)
            matrix = route[...]
            for i in range(tile // 16):
                halves = []
                for h in range(2):
                    at = 16 * i + 8 * h
                    piece = term[:, pl.ds(base + at, 8), :].reshape(tall, width).astype(BF16)
                    halves.append((nn(matrix, piece) * inv_root).reshape(ys, zs, 8, width))
                both = jnp.concatenate(halves, axis=2).astype(BF16)
                part[it][k, :, :, 16 * i : 16 * i + 16, :] = both
            for d in range(1, ys):
                y_copy(it, k, d).start()

            @pl.when(k >= lag)
            def _():
                z_phase(it, k - lag)

            return carry

        if it > 0:
            for k in range(slabs):
                half = nn(slow[k].reshape(terms * rows, width), vec[it]).astype(BF16)
                mixed[:, k * rows : (k + 1) * rows, :] = half.reshape(terms, rows, width)
            for w in range(terms):
                term[w] = nn(mixed[w], fast[w])
        lax.fori_loop(0, SLABS[it], body, 0)
        for k in range(SLABS[it] - lag, SLABS[it]):
            z_phase(it, k)
        for k in range(SLABS[it]):
            for d in range(1, zs):
                z_copy(it, k, d).wait_recv()
            added = zsum[it][k, my_z].astype(F32)
            for d in range(1, zs):
                added = added + z_in[it][k, d - 1].astype(F32)
            result[it, k * tile : (k + 1) * tile, :] = added
        source = vec[it].astype(F32)
        value = jnp.where(keep, result[it] + diag_frame.astype(F32) * source, 0.0)
        result[it] = value

    fast_copy.wait_recv()
    apply(0)
    first = result[0]
    vec[1] = first.astype(BF16)
    start = vec[0].astype(F32)
    scalar_start(1, [total(start * start), total(start * first), total(first * first)])
    apply(1)
    vv, vh, hh = scalar_finish(1, 3)
    energy = vh / vv
    near = 1.0 + STEP * energy
    scale = jnp.sqrt(cells / jnp.maximum(near * near * vv - 2.0 * STEP * near * vh + STEP * STEP * hh, vv))
    start = vec[0].astype(F32)
    first = result[0]
    x = scale * near * start - scale * STEP * first
    applied = scale * near * first - scale * STEP * result[1]
    y = applied - energy * x
    result[0] = x
    result[1] = y
    scalar_start(2, [total(x * x), total(x * y), total(y * y)])
    xx, xy, yy = scalar_finish(2, 3)
    gap = xy / xx
    norm = xx + STEP * STEP * jnp.maximum(yy - gap * xy, 0.0)
    grow = jnp.sqrt(cells / norm)
    bond = (grow * (result[0] - STEP * (result[1] - gap * result[0]))).astype(BF16)

    @pl.when(even)
    def _():
        bond_ref[...] = bond

    @pl.when(jnp.logical_not(even))
    def _():
        bond_ref[...] = nt(unit[...], bond).astype(BF16)

    energy_ref[...] = jnp.broadcast_to(energy + gap, (1, 128))

    for which in range(3):
        for d in range(1, sectors):
            scalar_copy(which, d).wait_send()
    fast_copy.wait_send()

    @pl.when(inner)
    def _():
        for k in range(slabs):
            slow_copy(k).wait_send()

    for it in range(ITERS):
        for k in range(SLABS[it]):
            for d in range(1, ys):
                y_copy(it, k, d).wait_send()
            for d in range(1, zs):
                z_copy(it, k, d).wait_send()


def local(regions, ys, zs, psi, left_env, right_env, diagonal, lc, rc, mask, target, size):
    width, terms = psi.shape[-1], left_env.shape[2]
    sectors, slabs = ys * zs, SLABS[0]
    rows = width // slabs
    y_peers, z_peers = max(ys - 1, 1), max(zs - 1, 1)
    envs = (terms, width, width)
    vmem = pl.BlockSpec(memory_space=pltpu.VMEM)
    smem = pl.BlockSpec(memory_space=pltpu.SMEM)
    hbm = pl.BlockSpec(memory_space=pl.ANY)
    dma = pltpu.SemaphoreType.DMA
    bond, energy, _, _ = pl.pallas_call(
        functools.partial(kernel, regions, ys, zs, width, terms),
        out_shape=(
            jax.ShapeDtypeStruct((width, width), BF16),
            jax.ShapeDtypeStruct((1, 128), F32),
            jax.ShapeDtypeStruct((slabs, terms, rows, width), BF16),
            jax.ShapeDtypeStruct((slabs, terms, rows, width), BF16),
        ),
        in_specs=[vmem, hbm, hbm, vmem, vmem, vmem, vmem, smem, smem],
        out_specs=(vmem, vmem, hbm, hbm),
        scratch_shapes=[
            pltpu.VMEM((2,) + envs, BF16),
            pltpu.VMEM(envs, BF16),
            pltpu.VMEM((2, width, width), BF16),
            pltpu.VMEM((slabs, terms, rows, width), BF16),
            pltpu.VMEM(envs, BF16),
            pltpu.VMEM((slabs, terms, rows, width), BF16),
            pltpu.VMEM(envs, BF16),
            pltpu.VMEM((2, width, width), BF16),
            pltpu.VMEM((width, width), BF16),
            pltpu.VMEM((sectors * 8, terms * 8), BF16),
            pltpu.VMEM((terms, width, width), F32),
            *[pltpu.VMEM((n, ys, zs, width // n, width), BF16) for n in SLABS],
            *[pltpu.VMEM((n, y_peers, zs, width // n, width), BF16) for n in SLABS],
            *[pltpu.VMEM((n, zs, width // n, width), BF16) for n in SLABS],
            *[pltpu.VMEM((n, z_peers, width // n, width), BF16) for n in SLABS],
            pltpu.VMEM((2, width, width), F32),
            pltpu.VMEM((3, sectors, 8, 128), F32),
            dma((2,)),
            dma((2, slabs)),
            dma((slabs,)),
            dma((slabs,)),
            dma((2,)),
            dma((ITERS, slabs, y_peers)),
            dma((ITERS, slabs, y_peers)),
            dma((ITERS, slabs, z_peers)),
            dma((ITERS, slabs, z_peers)),
            dma((3, sectors - 1)),
            dma((3, sectors - 1)),
        ],
        compiler_params=pltpu.CompilerParams(
            collective_id=0, has_side_effects=True, vmem_limit_bytes=56 * 2**20
        ),
    )(
        psi.reshape(width, width), left_env.reshape(envs), right_env.reshape(envs),
        diagonal.reshape(width, width), lc, rc, mask, target, size,
    )
    return bond.reshape(1, 1, width, width), energy[0, :1]


def solution(mesh):
    regions, sectors = mesh.shape["region"], mesh.shape["sector"]
    ys = 1
    while (2 * ys) * (2 * ys) * 2 <= sectors:
        ys *= 2
    in_specs = (
        P("region", "sector", None, None),
        P("region", "sector", None, None, None),
        P("region", "sector", None, None, None),
        P("region", "sector", None, None),
        P(),
        P(),
        P(),
        P("sector", None),
        P("sector"),
    )
    out_specs = (P("region", "sector", None, None), P("region"))
    body = functools.partial(local, regions, ys, sectors // ys)
    return jax.shard_map(body, mesh=mesh, in_specs=in_specs, out_specs=out_specs, check_vma=False)
```

```python
import functools
import math

import jax
import jax.numpy as jnp
from jax import lax
from jax.experimental import pallas as pl
from jax.experimental.pallas import tpu as pltpu
from jax.sharding import PartitionSpec as P

ITERS = 2
STEP = 0.5
SLABS = (4, 4)
LAGS = (1, 2)
F32 = jnp.float32
BF16 = jnp.bfloat16
MESH = pl.DeviceIdType.MESH


def nn(a, b):
    return lax.dot_general(a, b, (((1,), (0,)), ((), ())), preferred_element_type=F32)


def nt(a, b):
    return lax.dot_general(a, b, (((1,), (1,)), ((), ())), preferred_element_type=F32)


def iota(shape, dim):
    return lax.broadcasted_iota(jnp.int32, shape, dim)


def total(x):
    return jnp.sum(jnp.sum(x, axis=0, keepdims=True), axis=1, keepdims=True)


def kernel(
    regions, ys, zs, width, terms,
    psi_ref, left_hbm, right_hbm, diag_ref, lc_ref, rc_ref, mask_ref, target_ref, size_ref,
    bond_ref, energy_ref,
    env, mixed, frame, peer_frame, raw, norms, out_slow, slow, fast, vec, unit, route,
    term, part0, part1, y_in0, y_in1, zsum0, zsum1, z_in0, z_in1, result, scal,
    load_sem, slow_send, slow_recv, pair_send, pair_recv, y_send, y_recv, z_send, z_recv, s_send, s_recv,
):
    sectors = ys * zs
    part, y_in = (part0, part1), (y_in0, y_in1)
    zsum, z_in = (zsum0, zsum1), (z_in0, z_in1)
    slabs = SLABS[0]
    rows = width // slabs
    cells = float(sectors * width * width)
    region = lax.axis_index("region")
    me = lax.axis_index("sector")
    my_y, my_z = lax.rem(me, ys), lax.div(me, ys)
    odd = lax.rem(region, 2)
    even = odd == 0
    fast_peer = region + 1 - 2 * odd
    slow_peer = region - 1 + 2 * odd
    inner = jnp.logical_and(slow_peer >= 0, slow_peer < regions)
    edge = jnp.logical_not(inner)

    barrier = pltpu.get_barrier_semaphore()
    for d in range(1, sectors):
        pl.semaphore_signal(
            barrier, inc=1, device_id={"sector": lax.rem(me + d, sectors)}, device_id_type=MESH
        )
    pl.semaphore_signal(barrier, inc=1, device_id={"region": fast_peer}, device_id_type=MESH)

    @pl.when(inner)
    def _():
        pl.semaphore_signal(barrier, inc=1, device_id={"region": slow_peer}, device_id_type=MESH)

    def load(source, slot):
        return pltpu.make_async_copy(source, env.at[slot], load_sem.at[slot])

    @pl.when(even)
    def _():
        load(right_hbm, 0).start()

    @pl.when(jnp.logical_not(even))
    def _():
        load(left_hbm, 0).start()

    size = size_ref[0]
    square = (width, width)
    keep = jnp.logical_and(iota(square, 0) < size, iota(square, 1) < size)
    unit[...] = jnp.where(iota(square, 0) == iota(square, 1), 1.0, 0.0).astype(BF16)
    wide = jnp.where(keep, psi_ref[...].astype(F32), 0.0)
    masked = wide.astype(BF16)
    turned = nt(unit[...], masked).astype(BF16)

    @pl.when(even)
    def _():
        frame[0] = masked
        frame[1] = turned

    @pl.when(jnp.logical_not(even))
    def _():
        frame[0] = turned
        frame[1] = masked

    lanes = iota((8, 128), 1)

    def scalar_copy(which, d):
        peer = lax.rem(me + d, sectors)
        return pltpu.make_async_remote_copy(
            src_ref=scal.at[which, me], dst_ref=scal.at[which, me],
            send_sem=s_send.at[which, d - 1], recv_sem=s_recv.at[which, d - 1],
            device_id={"sector": peer}, device_id_type=MESH,
        )

    def scalar_start(which, values):
        packed = jnp.zeros((8, 128), F32)
        for lane, value in enumerate(values):
            packed = jnp.where(lanes == lane, jnp.broadcast_to(value, (8, 128)), packed)
        scal[which, me] = packed
        for d in range(1, sectors):
            scalar_copy(which, d).start()

    def scalar_finish(which, count):
        for d in range(1, sectors):
            scalar_copy(which, d).wait_recv()
        added = jnp.sum(scal[which], axis=0)[0:1, :]
        return [
            jnp.sum(jnp.where(lanes[0:1] == lane, added, 0.0), axis=1, keepdims=True)
            for lane in range(count)
        ]

    pl.semaphore_wait(barrier, sectors + inner.astype(jnp.int32))

    scalar_start(0, [total(wide * wide)])

    def pair_copy(which, source, target):
        return pltpu.make_async_remote_copy(
            src_ref=source, dst_ref=target,
            send_sem=pair_send.at[which], recv_sem=pair_recv.at[which],
            device_id={"region": fast_peer}, device_id_type=MESH,
        )

    pair_copy(0, frame.at[1], peer_frame).start()

    @pl.when(even)
    def _():
        pair_copy(1, left_hbm, raw).start()

        @pl.when(edge)
        def _():
            load(left_hbm, 1).start()

    @pl.when(jnp.logical_not(even))
    def _():
        pair_copy(1, right_hbm, raw).start()

        @pl.when(edge)
        def _():
            load(right_hbm, 1).start()


    tall = 8 * terms
    spread = jnp.where((iota((tall, terms), 0) >> 3) == iota((tall, terms), 1), 1.0, 0.0).astype(BF16)
    same = (iota((tall, tall), 0) & 7) == (iota((tall, tall), 1) & 7)
    pattern = mask_ref[...].astype(F32)

    def mixer(coeff):
        over = nn(spread, (coeff * pattern).astype(BF16)).astype(BF16)
        return jnp.where(same, nt(over, spread), 0.0).astype(BF16)

    left_c, right_c = lc_ref[...], rc_ref[...]
    parity = odd.astype(F32)
    matrix_mix = mixer(right_c + parity * (left_c - right_c))
    wanted = (sectors * 8, tall)
    aim = jnp.zeros(wanted, jnp.int32)
    for w in range(terms):
        aim = jnp.where((iota(wanted, 1) >> 3) == w, target_ref[0, w], aim)
    block = iota(wanted, 0) >> 3
    z_bits = zs.bit_length() - 1
    mine = (block & (zs - 1)) * ys + (block >> z_bits)
    hit = jnp.logical_and(aim == mine, (iota(wanted, 0) & 7) == (iota(wanted, 1) & 7))
    route[...] = jnp.where(hit, 1.0, 0.0).astype(BF16)

    def mix(source):
        def body(i, carry):
            for j in range(4):
                start = pl.multiple_of(i * 64 + j * 16, 16)
                x = source[:, pl.ds(start, 16), :].astype(F32)
                halves = []
                for h in range(2):
                    piece = x[:, 8 * h : 8 * h + 8, :].reshape(tall, width).astype(BF16)
                    halves.append(nn(matrix_mix, piece).reshape(terms, 8, width))
                mixed[:, pl.ds(start, 16), :] = jnp.concatenate(halves, axis=1).astype(BF16)
            return carry

        lax.fori_loop(0, width // 64, body, 0)

    group = max(g for g in range(1, 10) if terms % g == 0)

    def carry_env(factor, ahead, rescale, store):
        def body(i, carry):
            for j in range(group):
                v = i * group + j
                a = factor[...]
                y = nn(a, mixed[v]).astype(BF16)
                first = jnp.where(ahead, a, y)
                second = jnp.where(ahead, y, a)
                store(v, (rescale * nt(first, second)).astype(BF16))
            return carry

        lax.fori_loop(0, terms // group, body, 0)

    def load_wait(slot):
        load(left_hbm, slot).wait()

    def slow_copy(k):
        return pltpu.make_async_remote_copy(
            src_ref=out_slow.at[k], dst_ref=slow.at[k],
            send_sem=slow_send.at[k], recv_sem=slow_recv.at[k],
            device_id={"region": slow_peer}, device_id_type=MESH,
        )

    load_wait(0)
    mix(env.at[0])
    (start_norm,) = scalar_finish(0, 1)
    rescale = sectors * width / start_norm

    def store_slow(v, value):
        for k in range(slabs):
            out_slow[k, v] = value[k * rows : (k + 1) * rows]

    norms[0] = jnp.broadcast_to(rescale, (8, 128))
    pair_copy(2, norms.at[0], norms.at[1]).start()
    carry_env(frame.at[0], even, rescale, store_slow)

    @pl.when(inner)
    def _():
        for k in range(slabs):
            slow_copy(k).start()

    def store_fast(v, value):
        fast[v] = value

    pair_copy(0, frame.at[1], peer_frame).wait_recv()
    pair_copy(1, left_hbm, raw).wait_recv()
    mix(raw)
    pair_copy(2, norms.at[0], norms.at[1]).wait_recv()
    carry_env(peer_frame, jnp.logical_not(even), norms[1][0:1, 0:1], store_fast)

    @pl.when(jnp.logical_and(edge, even))
    def _():
        load_wait(1)

        def body(v, carry):
            for k in range(slabs):
                slow[k, v] = env[1, v, k * rows : (k + 1) * rows, :]
            return carry

        lax.fori_loop(0, terms, body, 0)

    @pl.when(jnp.logical_and(edge, jnp.logical_not(even)))
    def _():
        load_wait(1)

        def body(v, carry):
            value = nt(unit[...], env[1, v]).astype(BF16)
            for k in range(slabs):
                slow[k, v] = value[k * rows : (k + 1) * rows]
            return carry

        lax.fori_loop(0, terms, body, 0)

    vec[0] = (frame[0].astype(F32) * jnp.sqrt(cells / start_norm)).astype(BF16)
    diag = diag_ref[...]
    diag_frame = jnp.where(even, diag, nt(unit[...], diag).astype(BF16))
    inv_root = 1.0 / math.sqrt(terms)

    def y_copy(it, k, d):
        peer_y = lax.rem(my_y + d, ys)
        return pltpu.make_async_remote_copy(
            src_ref=part[it].at[k, peer_y], dst_ref=y_in[it].at[k, d - 1],
            send_sem=y_send.at[it, k, d - 1], recv_sem=y_recv.at[it, k, d - 1],
            device_id={"sector": my_z * ys + peer_y}, device_id_type=MESH,
        )

    def z_copy(it, k, d):
        peer_z = lax.rem(my_z + d, zs)
        return pltpu.make_async_remote_copy(
            src_ref=zsum[it].at[k, peer_z], dst_ref=z_in[it].at[k, d - 1],
            send_sem=z_send.at[it, k, d - 1], recv_sem=z_recv.at[it, k, d - 1],
            device_id={"sector": peer_z * ys + my_y}, device_id_type=MESH,
        )

    def z_phase(it, k):
        for d in range(1, ys):
            y_copy(it, k, d).wait_recv()
        added = part[it][k, my_y].astype(F32)
        for d in range(1, ys):
            added = added + y_in[it][k, d - 1].astype(F32)
        zsum[it][k] = added.astype(BF16)
        for d in range(1, zs):
            z_copy(it, k, d).start()

    def apply(it):
        merge = slabs // SLABS[it]
        tile = merge * rows

        lag = LAGS[it]

        def body(k, carry):
            if it == 0:
                @pl.when(inner)
                def _():
                    slow_copy(k).wait_recv()

            left = slow[pl.ds(k * merge, merge)].reshape(merge * terms * rows, width)
            half = nn(left, vec[it]).astype(BF16)
            for w in range(terms):
                pieces = [
                    half[(j * terms + w) * rows : (j * terms + w + 1) * rows] for j in range(merge)
                ]
                term[w, 0:tile, :] = nn(jnp.concatenate(pieces, axis=0), fast[w])
            matrix = route[...]
            for i in range(tile // 16):
                halves = []
                for h in range(2):
                    at = 16 * i + 8 * h
                    piece = term[:, at : at + 8, :].reshape(tall, width).astype(BF16)
                    halves.append((nn(matrix, piece) * inv_root).reshape(ys, zs, 8, width))
                both = jnp.concatenate(halves, axis=2).astype(BF16)
                part[it][k, :, :, 16 * i : 16 * i + 16, :] = both
            for d in range(1, ys):
                y_copy(it, k, d).start()

            @pl.when(k >= lag)
            def _():
                z_phase(it, k - lag)

            return carry

        lax.fori_loop(0, SLABS[it], body, 0)
        for k in range(SLABS[it] - lag, SLABS[it]):
            z_phase(it, k)
        for k in range(SLABS[it]):
            for d in range(1, zs):
                z_copy(it, k, d).wait_recv()
            added = zsum[it][k, my_z].astype(F32)
            for d in range(1, zs):
                added = added + z_in[it][k, d - 1].astype(F32)
            result[it, k * tile : (k + 1) * tile, :] = added
        source = vec[it].astype(F32)
        value = jnp.where(keep, result[it] + diag_frame.astype(F32) * source, 0.0)
        result[it] = value

    apply(0)
    first = result[0]
    vec[1] = first.astype(BF16)
    start = vec[0].astype(F32)
    scalar_start(1, [total(start * start), total(start * first), total(first * first)])
    apply(1)
    vv, vh, hh = scalar_finish(1, 3)
    energy = vh / vv
    near = 1.0 + STEP * energy
    scale = jnp.sqrt(cells / jnp.maximum(near * near * vv - 2.0 * STEP * near * vh + STEP * STEP * hh, vv))
    start = vec[0].astype(F32)
    first = result[0]
    x = scale * near * start - scale * STEP * first
    applied = scale * near * first - scale * STEP * result[1]
    y = applied - energy * x
    result[0] = x
    result[1] = y
    scalar_start(2, [total(x * x), total(x * y), total(y * y)])
    xx, xy, yy = scalar_finish(2, 3)
    gap = xy / xx
    norm = xx + STEP * STEP * jnp.maximum(yy - gap * xy, 0.0)
    grow = jnp.sqrt(cells / norm)
    bond = (grow * (result[0] - STEP * (result[1] - gap * result[0]))).astype(BF16)

    @pl.when(even)
    def _():
        bond_ref[...] = bond

    @pl.when(jnp.logical_not(even))
    def _():
        bond_ref[...] = nt(unit[...], bond).astype(BF16)

    energy_ref[...] = jnp.broadcast_to(energy + gap, (1, 128))

    for which in range(3):
        for d in range(1, sectors):
            scalar_copy(which, d).wait_send()
    pair_copy(0, frame.at[1], peer_frame).wait_send()
    pair_copy(1, left_hbm, raw).wait_send()
    pair_copy(2, norms.at[0], norms.at[1]).wait_send()

    @pl.when(inner)
    def _():
        for k in range(slabs):
            slow_copy(k).wait_send()

    for it in range(ITERS):
        for k in range(SLABS[it]):
            for d in range(1, ys):
                y_copy(it, k, d).wait_send()
            for d in range(1, zs):
                z_copy(it, k, d).wait_send()


def local(regions, ys, zs, psi, left_env, right_env, diagonal, lc, rc, mask, target, size):
    width, terms = psi.shape[-1], left_env.shape[2]
    sectors, slabs = ys * zs, SLABS[0]
    rows, tiles = width // slabs, [width // n for n in SLABS]
    y_peers, z_peers = max(ys - 1, 1), max(zs - 1, 1)
    envs = (terms, width, width)
    vmem = pl.BlockSpec(memory_space=pltpu.VMEM)
    smem = pl.BlockSpec(memory_space=pltpu.SMEM)
    hbm = pl.BlockSpec(memory_space=pl.ANY)
    dma = pltpu.SemaphoreType.DMA
    bond, energy = pl.pallas_call(
        functools.partial(kernel, regions, ys, zs, width, terms),
        out_shape=(
            jax.ShapeDtypeStruct((width, width), BF16),
            jax.ShapeDtypeStruct((1, 128), F32),
        ),
        in_specs=[vmem, hbm, hbm, vmem, vmem, vmem, vmem, smem, smem],
        out_specs=(vmem, vmem),
        scratch_shapes=[
            pltpu.VMEM((2,) + envs, BF16),
            pltpu.VMEM(envs, BF16),
            pltpu.VMEM((2, width, width), BF16),
            pltpu.VMEM((width, width), BF16),
            pltpu.VMEM(envs, BF16),
            pltpu.VMEM((2, 8, 128), F32),
            pltpu.VMEM((slabs, terms, rows, width), BF16),
            pltpu.VMEM((slabs, terms, rows, width), BF16),
            pltpu.VMEM(envs, BF16),
            pltpu.VMEM((2, width, width), BF16),
            pltpu.VMEM((width, width), BF16),
            pltpu.VMEM((sectors * 8, terms * 8), BF16),
            pltpu.VMEM((terms, max(tiles), width), F32),
            *[pltpu.VMEM((n, ys, zs, width // n, width), BF16) for n in SLABS],
            *[pltpu.VMEM((n, y_peers, zs, width // n, width), BF16) for n in SLABS],
            *[pltpu.VMEM((n, zs, width // n, width), BF16) for n in SLABS],
            *[pltpu.VMEM((n, z_peers, width // n, width), BF16) for n in SLABS],
            pltpu.VMEM((2, width, width), F32),
            pltpu.VMEM((3, sectors, 8, 128), F32),
            dma((2,)),
            dma((slabs,)),
            dma((slabs,)),
            dma((3,)),
            dma((3,)),
            dma((ITERS, slabs, y_peers)),
            dma((ITERS, slabs, y_peers)),
            dma((ITERS, slabs, z_peers)),
            dma((ITERS, slabs, z_peers)),
            dma((3, sectors - 1)),
            dma((3, sectors - 1)),
        ],
        compiler_params=pltpu.CompilerParams(
            collective_id=0, has_side_effects=True, vmem_limit_bytes=56 * 2**20
        ),
    )(
        psi.reshape(width, width), left_env.reshape(envs), right_env.reshape(envs),
        diagonal.reshape(width, width), lc, rc, mask, target, size,
    )
    return bond.reshape(1, 1, width, width), energy[0, :1]


def solution(mesh):
    regions, sectors = mesh.shape["region"], mesh.shape["sector"]
    ys = 1
    while (2 * ys) * (2 * ys) * 2 <= sectors:
        ys *= 2
    in_specs = (
        P("region", "sector", None, None),
        P("region", "sector", None, None, None),
        P("region", "sector", None, None, None),
        P("region", "sector", None, None),
        P(),
        P(),
        P(),
        P("sector", None),
        P("sector"),
    )
    out_specs = (P("region", "sector", None, None), P("region"))
    body = functools.partial(local, regions, ys, sectors // ys)
    return jax.shard_map(body, mesh=mesh, in_specs=in_specs, out_specs=out_specs, check_vma=False)
```

```python
import functools
import math

import jax
import jax.numpy as jnp
from jax import lax
from jax.experimental import pallas as pl
from jax.experimental.pallas import tpu as pltpu
from jax.sharding import PartitionSpec as P

ITERS = 2
STEP = 0.5
SLABS = (4, 4)
LAGS = (1, 2)
F32 = jnp.float32
BF16 = jnp.bfloat16
MESH = pl.DeviceIdType.MESH


def nn(a, b):
    return lax.dot_general(a, b, (((1,), (0,)), ((), ())), preferred_element_type=F32)


def nt(a, b):
    return lax.dot_general(a, b, (((1,), (1,)), ((), ())), preferred_element_type=F32)


def iota(shape, dim):
    return lax.broadcasted_iota(jnp.int32, shape, dim)


def total(x):
    return jnp.sum(jnp.sum(x, axis=0, keepdims=True), axis=1, keepdims=True)


def kernel(
    regions, ys, zs, width, terms,
    psi_ref, left_hbm, right_hbm, diag_ref, lc_ref, rc_ref, mask_ref, target_ref, size_ref,
    bond_ref, energy_ref,
    env, mixed, frame, peer_frame, raw, norms, out_slow, slow, fast, vec, unit, route,
    term, part0, part1, y_in0, y_in1, zsum0, zsum1, z_in0, z_in1, result, scal,
    load_sem, slow_send, slow_recv, pair_send, pair_recv, y_send, y_recv, z_send, z_recv, s_send, s_recv,
):
    sectors = ys * zs
    part, y_in = (part0, part1), (y_in0, y_in1)
    zsum, z_in = (zsum0, zsum1), (z_in0, z_in1)
    slabs = SLABS[0]
    rows = width // slabs
    cells = float(sectors * width * width)
    region = lax.axis_index("region")
    me = lax.axis_index("sector")
    my_y, my_z = lax.rem(me, ys), lax.div(me, ys)
    odd = lax.rem(region, 2)
    even = odd == 0
    fast_peer = region + 1 - 2 * odd
    slow_peer = region - 1 + 2 * odd
    inner = jnp.logical_and(slow_peer >= 0, slow_peer < regions)
    edge = jnp.logical_not(inner)

    barrier = pltpu.get_barrier_semaphore()
    for d in range(1, sectors):
        pl.semaphore_signal(
            barrier, inc=1, device_id={"sector": lax.rem(me + d, sectors)}, device_id_type=MESH
        )
    pl.semaphore_signal(barrier, inc=1, device_id={"region": fast_peer}, device_id_type=MESH)

    @pl.when(inner)
    def _():
        pl.semaphore_signal(barrier, inc=1, device_id={"region": slow_peer}, device_id_type=MESH)

    def load(source, slot):
        return pltpu.make_async_copy(source, env.at[slot], load_sem.at[slot])

    @pl.when(even)
    def _():
        load(right_hbm, 0).start()

    @pl.when(jnp.logical_not(even))
    def _():
        load(left_hbm, 0).start()

    size = size_ref[0]
    square = (width, width)
    keep = jnp.logical_and(iota(square, 0) < size, iota(square, 1) < size)
    unit[...] = jnp.where(iota(square, 0) == iota(square, 1), 1.0, 0.0).astype(BF16)
    wide = jnp.where(keep, psi_ref[...].astype(F32), 0.0)
    masked = wide.astype(BF16)
    turned = nt(unit[...], masked).astype(BF16)

    @pl.when(even)
    def _():
        frame[0] = masked
        frame[1] = turned

    @pl.when(jnp.logical_not(even))
    def _():
        frame[0] = turned
        frame[1] = masked

    lanes = iota((8, 128), 1)

    def scalar_copy(which, d):
        peer = lax.rem(me + d, sectors)
        return pltpu.make_async_remote_copy(
            src_ref=scal.at[which, me], dst_ref=scal.at[which, me],
            send_sem=s_send.at[which, d - 1], recv_sem=s_recv.at[which, d - 1],
            device_id={"sector": peer}, device_id_type=MESH,
        )

    def scalar_start(which, values):
        packed = jnp.zeros((8, 128), F32)
        for lane, value in enumerate(values):
            packed = jnp.where(lanes == lane, jnp.broadcast_to(value, (8, 128)), packed)
        scal[which, me] = packed
        for d in range(1, sectors):
            scalar_copy(which, d).start()

    def scalar_finish(which, count):
        for d in range(1, sectors):
            scalar_copy(which, d).wait_recv()
        added = jnp.sum(scal[which], axis=0)[0:1, :]
        return [
            jnp.sum(jnp.where(lanes[0:1] == lane, added, 0.0), axis=1, keepdims=True)
            for lane in range(count)
        ]

    pl.semaphore_wait(barrier, sectors + inner.astype(jnp.int32))

    scalar_start(0, [total(wide * wide)])

    def pair_copy(which, source, target):
        return pltpu.make_async_remote_copy(
            src_ref=source, dst_ref=target,
            send_sem=pair_send.at[which], recv_sem=pair_recv.at[which],
            device_id={"region": fast_peer}, device_id_type=MESH,
        )

    pair_copy(0, frame.at[1], peer_frame.at[0]).start()

    @pl.when(even)
    def _():
        pair_copy(1, left_hbm, raw).start()

        @pl.when(edge)
        def _():
            load(left_hbm, 1).start()

    @pl.when(jnp.logical_not(even))
    def _():
        pair_copy(1, right_hbm, raw).start()

        @pl.when(edge)
        def _():
            load(right_hbm, 1).start()


    tall = 8 * terms
    spread = jnp.where((iota((tall, terms), 0) >> 3) == iota((tall, terms), 1), 1.0, 0.0).astype(BF16)
    same = (iota((tall, tall), 0) & 7) == (iota((tall, tall), 1) & 7)
    pattern = mask_ref[...].astype(F32)

    def mixer(coeff):
        over = nn(spread, (coeff * pattern).astype(BF16)).astype(BF16)
        return jnp.where(same, nt(over, spread), 0.0).astype(BF16)

    left_c, right_c = lc_ref[...], rc_ref[...]
    parity = odd.astype(F32)
    matrix_mix = mixer(right_c + parity * (left_c - right_c))
    wanted = (sectors * 8, tall)
    aim = jnp.zeros(wanted, jnp.int32)
    for w in range(terms):
        aim = jnp.where((iota(wanted, 1) >> 3) == w, target_ref[0, w], aim)
    block = iota(wanted, 0) >> 3
    z_bits = zs.bit_length() - 1
    mine = (block & (zs - 1)) * ys + (block >> z_bits)
    hit = jnp.logical_and(aim == mine, (iota(wanted, 0) & 7) == (iota(wanted, 1) & 7))
    route[...] = jnp.where(hit, 1.0, 0.0).astype(BF16)

    def mix(source, factor):
        right = factor[...]

        def body(i, carry):
            for j in range(4):
                start = pl.multiple_of(i * 64 + j * 16, 16)
                x = source[:, pl.ds(start, 16), :].astype(F32)
                halves = []
                for h in range(2):
                    piece = x[:, 8 * h : 8 * h + 8, :].reshape(tall, width).astype(BF16)
                    halves.append(nn(matrix_mix, piece).reshape(terms, 8, width))
                both = jnp.concatenate(halves, axis=1).astype(BF16).reshape(16 * terms, width)
                mixed[:, pl.ds(start, 16), :] = nn(both, right).astype(BF16).reshape(terms, 16, width)
            return carry

        lax.fori_loop(0, width // 64, body, 0)

    group = max(g for g in range(1, 10) if terms % g == 0)

    def carry_env(factor, ahead, rescale, store):
        def run(turn):
            def body(i, carry):
                for j in range(group):
                    v = i * group + j
                    value = rescale * nn(factor[...], mixed[v])
                    store(v, (value.T if turn else value).astype(BF16))
                return carry

            lax.fori_loop(0, terms // group, body, 0)

        @pl.when(ahead)
        def _():
            run(True)

        @pl.when(jnp.logical_not(ahead))
        def _():
            run(False)

    def load_wait(slot):
        load(left_hbm, slot).wait()

    def slow_copy(k):
        return pltpu.make_async_remote_copy(
            src_ref=out_slow.at[k], dst_ref=slow.at[k],
            send_sem=slow_send.at[k], recv_sem=slow_recv.at[k],
            device_id={"region": slow_peer}, device_id_type=MESH,
        )

    load_wait(0)
    mix(env.at[0], frame.at[1])
    (start_norm,) = scalar_finish(0, 1)
    rescale = sectors * width / start_norm

    def store_slow(v, value):
        for k in range(slabs):
            out_slow[k, v] = value[k * rows : (k + 1) * rows]

    norms[0] = jnp.broadcast_to(rescale, (8, 128))
    pair_copy(2, norms.at[0], norms.at[1]).start()
    carry_env(frame.at[0], even, rescale, store_slow)

    @pl.when(inner)
    def _():
        for k in range(slabs):
            slow_copy(k).start()

    def store_fast(v, value):
        fast[v] = value

    pair_copy(0, frame.at[1], peer_frame.at[0]).wait_recv()
    pair_copy(1, left_hbm, raw).wait_recv()
    peer_frame[1] = nt(unit[...], peer_frame[0]).astype(BF16)
    mix(raw, peer_frame.at[1])
    pair_copy(2, norms.at[0], norms.at[1]).wait_recv()
    carry_env(peer_frame.at[0], jnp.logical_not(even), norms[1][0:1, 0:1], store_fast)

    @pl.when(jnp.logical_and(edge, even))
    def _():
        load_wait(1)

        def body(v, carry):
            for k in range(slabs):
                slow[k, v] = env[1, v, k * rows : (k + 1) * rows, :]
            return carry

        lax.fori_loop(0, terms, body, 0)

    @pl.when(jnp.logical_and(edge, jnp.logical_not(even)))
    def _():
        load_wait(1)

        def body(v, carry):
            value = nt(unit[...], env[1, v]).astype(BF16)
            for k in range(slabs):
                slow[k, v] = value[k * rows : (k + 1) * rows]
            return carry

        lax.fori_loop(0, terms, body, 0)

    vec[0] = (frame[0].astype(F32) * jnp.sqrt(cells / start_norm)).astype(BF16)
    diag = diag_ref[...]
    diag_frame = jnp.where(even, diag, nt(unit[...], diag).astype(BF16))
    inv_root = 1.0 / math.sqrt(terms)

    def y_copy(it, k, d):
        peer_y = lax.rem(my_y + d, ys)
        return pltpu.make_async_remote_copy(
            src_ref=part[it].at[k, peer_y], dst_ref=y_in[it].at[k, d - 1],
            send_sem=y_send.at[it, k, d - 1], recv_sem=y_recv.at[it, k, d - 1],
            device_id={"sector": my_z * ys + peer_y}, device_id_type=MESH,
        )

    def z_copy(it, k, d):
        peer_z = lax.rem(my_z + d, zs)
        return pltpu.make_async_remote_copy(
            src_ref=zsum[it].at[k, peer_z], dst_ref=z_in[it].at[k, d - 1],
            send_sem=z_send.at[it, k, d - 1], recv_sem=z_recv.at[it, k, d - 1],
            device_id={"sector": peer_z * ys + my_y}, device_id_type=MESH,
        )

    def z_phase(it, k):
        for d in range(1, ys):
            y_copy(it, k, d).wait_recv()
        added = part[it][k, my_y].astype(F32)
        for d in range(1, ys):
            added = added + y_in[it][k, d - 1].astype(F32)
        zsum[it][k] = added.astype(BF16)
        for d in range(1, zs):
            z_copy(it, k, d).start()

    def apply(it):
        merge = slabs // SLABS[it]
        tile = merge * rows

        lag = LAGS[it]

        def body(k, carry):
            if it == 0:
                @pl.when(inner)
                def _():
                    slow_copy(k).wait_recv()

            left = slow[pl.ds(k * merge, merge)].reshape(merge * terms * rows, width)
            half = nn(left, vec[it]).astype(BF16)
            for w in range(terms):
                pieces = [
                    half[(j * terms + w) * rows : (j * terms + w + 1) * rows] for j in range(merge)
                ]
                term[w, 0:tile, :] = nn(jnp.concatenate(pieces, axis=0), fast[w])
            matrix = route[...]
            for i in range(tile // 16):
                halves = []
                for h in range(2):
                    at = 16 * i + 8 * h
                    piece = term[:, at : at + 8, :].reshape(tall, width).astype(BF16)
                    halves.append((nn(matrix, piece) * inv_root).reshape(ys, zs, 8, width))
                both = jnp.concatenate(halves, axis=2).astype(BF16)
                part[it][k, :, :, 16 * i : 16 * i + 16, :] = both
            for d in range(1, ys):
                y_copy(it, k, d).start()

            @pl.when(k >= lag)
            def _():
                z_phase(it, k - lag)

            return carry

        lax.fori_loop(0, SLABS[it], body, 0)
        for k in range(SLABS[it] - lag, SLABS[it]):
            z_phase(it, k)
        for k in range(SLABS[it]):
            for d in range(1, zs):
                z_copy(it, k, d).wait_recv()
            added = zsum[it][k, my_z].astype(F32)
            for d in range(1, zs):
                added = added + z_in[it][k, d - 1].astype(F32)
            result[it, k * tile : (k + 1) * tile, :] = added
        source = vec[it].astype(F32)
        value = jnp.where(keep, result[it] + diag_frame.astype(F32) * source, 0.0)
        result[it] = value

    apply(0)
    first = result[0]
    vec[1] = first.astype(BF16)
    start = vec[0].astype(F32)
    scalar_start(1, [total(start * start), total(start * first), total(first * first)])
    apply(1)
    vv, vh, hh = scalar_finish(1, 3)
    energy = vh / vv
    near = 1.0 + STEP * energy
    scale = jnp.sqrt(cells / jnp.maximum(near * near * vv - 2.0 * STEP * near * vh + STEP * STEP * hh, vv))
    start = vec[0].astype(F32)
    first = result[0]
    x = scale * near * start - scale * STEP * first
    applied = scale * near * first - scale * STEP * result[1]
    y = applied - energy * x
    result[0] = x
    result[1] = y
    scalar_start(2, [total(x * x), total(x * y), total(y * y)])
    xx, xy, yy = scalar_finish(2, 3)
    gap = xy / xx
    norm = xx + STEP * STEP * jnp.maximum(yy - gap * xy, 0.0)
    grow = jnp.sqrt(cells / norm)
    bond = (grow * (result[0] - STEP * (result[1] - gap * result[0]))).astype(BF16)

    @pl.when(even)
    def _():
        bond_ref[...] = bond

    @pl.when(jnp.logical_not(even))
    def _():
        bond_ref[...] = nt(unit[...], bond).astype(BF16)

    energy_ref[...] = jnp.broadcast_to(energy + gap, (1, 128))

    for which in range(3):
        for d in range(1, sectors):
            scalar_copy(which, d).wait_send()
    pair_copy(0, frame.at[1], peer_frame.at[0]).wait_send()
    pair_copy(1, left_hbm, raw).wait_send()
    pair_copy(2, norms.at[0], norms.at[1]).wait_send()

    @pl.when(inner)
    def _():
        for k in range(slabs):
            slow_copy(k).wait_send()

    for it in range(ITERS):
        for k in range(SLABS[it]):
            for d in range(1, ys):
                y_copy(it, k, d).wait_send()
            for d in range(1, zs):
                z_copy(it, k, d).wait_send()


def local(regions, ys, zs, psi, left_env, right_env, diagonal, lc, rc, mask, target, size):
    width, terms = psi.shape[-1], left_env.shape[2]
    sectors, slabs = ys * zs, SLABS[0]
    rows, tiles = width // slabs, [width // n for n in SLABS]
    y_peers, z_peers = max(ys - 1, 1), max(zs - 1, 1)
    envs = (terms, width, width)
    vmem = pl.BlockSpec(memory_space=pltpu.VMEM)
    smem = pl.BlockSpec(memory_space=pltpu.SMEM)
    hbm = pl.BlockSpec(memory_space=pl.ANY)
    dma = pltpu.SemaphoreType.DMA
    bond, energy = pl.pallas_call(
        functools.partial(kernel, regions, ys, zs, width, terms),
        out_shape=(
            jax.ShapeDtypeStruct((width, width), BF16),
            jax.ShapeDtypeStruct((1, 128), F32),
        ),
        in_specs=[vmem, hbm, hbm, vmem, vmem, vmem, vmem, smem, smem],
        out_specs=(vmem, vmem),
        scratch_shapes=[
            pltpu.VMEM((2,) + envs, BF16),
            pltpu.VMEM(envs, BF16),
            pltpu.VMEM((2, width, width), BF16),
            pltpu.VMEM((2, width, width), BF16),
            pltpu.VMEM(envs, BF16),
            pltpu.VMEM((2, 8, 128), F32),
            pltpu.VMEM((slabs, terms, rows, width), BF16),
            pltpu.VMEM((slabs, terms, rows, width), BF16),
            pltpu.VMEM(envs, BF16),
            pltpu.VMEM((2, width, width), BF16),
            pltpu.VMEM((width, width), BF16),
            pltpu.VMEM((sectors * 8, terms * 8), BF16),
            pltpu.VMEM((terms, max(tiles), width), F32),
            *[pltpu.VMEM((n, ys, zs, width // n, width), BF16) for n in SLABS],
            *[pltpu.VMEM((n, y_peers, zs, width // n, width), BF16) for n in SLABS],
            *[pltpu.VMEM((n, zs, width // n, width), BF16) for n in SLABS],
            *[pltpu.VMEM((n, z_peers, width // n, width), BF16) for n in SLABS],
            pltpu.VMEM((2, width, width), F32),
            pltpu.VMEM((3, sectors, 8, 128), F32),
            dma((2,)),
            dma((slabs,)),
            dma((slabs,)),
            dma((3,)),
            dma((3,)),
            dma((ITERS, slabs, y_peers)),
            dma((ITERS, slabs, y_peers)),
            dma((ITERS, slabs, z_peers)),
            dma((ITERS, slabs, z_peers)),
            dma((3, sectors - 1)),
            dma((3, sectors - 1)),
        ],
        compiler_params=pltpu.CompilerParams(
            collective_id=0, has_side_effects=True, vmem_limit_bytes=56 * 2**20
        ),
    )(
        psi.reshape(width, width), left_env.reshape(envs), right_env.reshape(envs),
        diagonal.reshape(width, width), lc, rc, mask, target, size,
    )
    return bond.reshape(1, 1, width, width), energy[0, :1]


def solution(mesh):
    regions, sectors = mesh.shape["region"], mesh.shape["sector"]
    ys = 1
    while (2 * ys) * (2 * ys) * 2 <= sectors:
        ys *= 2
    in_specs = (
        P("region", "sector", None, None),
        P("region", "sector", None, None, None),
        P("region", "sector", None, None, None),
        P("region", "sector", None, None),
        P(),
        P(),
        P(),
        P("sector", None),
        P("sector"),
    )
    out_specs = (P("region", "sector", None, None), P("region"))
    body = functools.partial(local, regions, ys, sectors // ys)
    return jax.shard_map(body, mesh=mesh, in_specs=in_specs, out_specs=out_specs, check_vma=False)
```

```python
import functools
import math

import jax
import jax.numpy as jnp
from jax import lax
from jax.experimental import pallas as pl
from jax.experimental.pallas import tpu as pltpu
from jax.sharding import PartitionSpec as P

ITERS = 2
STEP = 0.5
SLABS = (4, 4)
LAGS = (1, 2)
F32 = jnp.float32
BF16 = jnp.bfloat16
MESH = pl.DeviceIdType.MESH


def nn(a, b):
    return lax.dot_general(a, b, (((1,), (0,)), ((), ())), preferred_element_type=F32)


def nt(a, b):
    return lax.dot_general(a, b, (((1,), (1,)), ((), ())), preferred_element_type=F32)


def iota(shape, dim):
    return lax.broadcasted_iota(jnp.int32, shape, dim)


def total(x):
    return jnp.sum(jnp.sum(x, axis=0, keepdims=True), axis=1, keepdims=True)


def kernel(
    regions, ys, zs, width, terms,
    psi_ref, left_hbm, right_hbm, diag_ref, lc_ref, rc_ref, mask_ref, target_ref, size_ref,
    bond_ref, energy_ref,
    env, mixed, frame, peer_frame, raw, norms, out_slow, slow, fast, vec, unit, route,
    term, part0, part1, y_in0, y_in1, zsum0, zsum1, z_in0, z_in1, result, scal,
    load_sem, slow_send, slow_recv, pair_send, pair_recv, y_send, y_recv, z_send, z_recv, s_send, s_recv,
):
    sectors = ys * zs
    part, y_in = (part0, part1), (y_in0, y_in1)
    zsum, z_in = (zsum0, zsum1), (z_in0, z_in1)
    slabs = SLABS[0]
    rows = width // slabs
    cells = float(sectors * width * width)
    region = lax.axis_index("region")
    me = lax.axis_index("sector")
    my_y, my_z = lax.rem(me, ys), lax.div(me, ys)
    odd = lax.rem(region, 2)
    even = odd == 0
    fast_peer = region + 1 - 2 * odd
    slow_peer = region - 1 + 2 * odd
    inner = jnp.logical_and(slow_peer >= 0, slow_peer < regions)
    edge = jnp.logical_not(inner)

    barrier = pltpu.get_barrier_semaphore()
    for d in range(1, sectors):
        pl.semaphore_signal(
            barrier, inc=1, device_id={"sector": lax.rem(me + d, sectors)}, device_id_type=MESH
        )
    pl.semaphore_signal(barrier, inc=1, device_id={"region": fast_peer}, device_id_type=MESH)

    @pl.when(inner)
    def _():
        pl.semaphore_signal(barrier, inc=1, device_id={"region": slow_peer}, device_id_type=MESH)

    def load(source, slot):
        return pltpu.make_async_copy(source, env.at[slot], load_sem.at[slot])

    @pl.when(even)
    def _():
        load(right_hbm, 0).start()

    @pl.when(jnp.logical_not(even))
    def _():
        load(left_hbm, 0).start()

    size = size_ref[0]
    square = (width, width)
    keep = jnp.logical_and(iota(square, 0) < size, iota(square, 1) < size)
    unit[...] = jnp.where(iota(square, 0) == iota(square, 1), 1.0, 0.0).astype(BF16)
    wide = jnp.where(keep, psi_ref[...].astype(F32), 0.0)
    masked = wide.astype(BF16)
    turned = nt(unit[...], masked).astype(BF16)

    @pl.when(even)
    def _():
        frame[0] = masked
        frame[1] = turned

    @pl.when(jnp.logical_not(even))
    def _():
        frame[0] = turned
        frame[1] = masked

    lanes = iota((8, 128), 1)

    def scalar_copy(which, d):
        peer = lax.rem(me + d, sectors)
        return pltpu.make_async_remote_copy(
            src_ref=scal.at[which, me], dst_ref=scal.at[which, me],
            send_sem=s_send.at[which, d - 1], recv_sem=s_recv.at[which, d - 1],
            device_id={"sector": peer}, device_id_type=MESH,
        )

    def scalar_start(which, values):
        packed = jnp.zeros((8, 128), F32)
        for lane, value in enumerate(values):
            packed = jnp.where(lanes == lane, jnp.broadcast_to(value, (8, 128)), packed)
        scal[which, me] = packed
        for d in range(1, sectors):
            scalar_copy(which, d).start()

    def scalar_finish(which, count):
        for d in range(1, sectors):
            scalar_copy(which, d).wait_recv()
        added = jnp.sum(scal[which], axis=0)[0:1, :]
        return [
            jnp.sum(jnp.where(lanes[0:1] == lane, added, 0.0), axis=1, keepdims=True)
            for lane in range(count)
        ]

    pl.semaphore_wait(barrier, sectors + inner.astype(jnp.int32))

    scalar_start(0, [total(wide * wide)])

    def pair_copy(which, source, target):
        return pltpu.make_async_remote_copy(
            src_ref=source, dst_ref=target,
            send_sem=pair_send.at[which], recv_sem=pair_recv.at[which],
            device_id={"region": fast_peer}, device_id_type=MESH,
        )

    pair_copy(0, frame.at[1], peer_frame.at[0]).start()

    @pl.when(even)
    def _():
        pair_copy(1, left_hbm, raw).start()

        @pl.when(edge)
        def _():
            load(left_hbm, 1).start()

    @pl.when(jnp.logical_not(even))
    def _():
        pair_copy(1, right_hbm, raw).start()

        @pl.when(edge)
        def _():
            load(right_hbm, 1).start()


    tall = 16 * terms
    spread = jnp.where((iota((tall, terms), 0) >> 4) == iota((tall, terms), 1), 1.0, 0.0).astype(BF16)
    same = (iota((tall, tall), 0) & 15) == (iota((tall, tall), 1) & 15)
    pattern = mask_ref[...].astype(F32)

    def mixer(coeff):
        over = nn(spread, (coeff * pattern).astype(BF16)).astype(BF16)
        return jnp.where(same, nt(over, spread), 0.0).astype(BF16)

    left_c, right_c = lc_ref[...], rc_ref[...]
    parity = odd.astype(F32)
    matrix_mix = mixer(right_c + parity * (left_c - right_c))
    wanted = (sectors * 16, tall)
    aim = jnp.zeros(wanted, jnp.int32)
    for w in range(terms):
        aim = jnp.where((iota(wanted, 1) >> 4) == w, target_ref[0, w], aim)
    block = iota(wanted, 0) >> 4
    z_bits = zs.bit_length() - 1
    mine = (block & (zs - 1)) * ys + (block >> z_bits)
    hit = jnp.logical_and(aim == mine, (iota(wanted, 0) & 15) == (iota(wanted, 1) & 15))
    route[...] = jnp.where(hit, 1.0, 0.0).astype(BF16)

    def mix(source, factor):
        right = factor[...]

        def body(i, carry):
            for j in range(4):
                start = pl.multiple_of(i * 64 + j * 16, 16)
                piece = source[:, pl.ds(start, 16), :].reshape(tall, width)
                both = nn(matrix_mix, piece).astype(BF16)
                mixed[:, pl.ds(start, 16), :] = nn(both, right).astype(BF16).reshape(terms, 16, width)
            return carry

        lax.fori_loop(0, width // 64, body, 0)

    group = max(g for g in range(1, 10) if terms % g == 0)

    def carry_env(factor, ahead, rescale, store):
        def run(turn):
            def body(i, carry):
                for j in range(group):
                    v = i * group + j
                    value = rescale * nn(factor[...], mixed[v])
                    store(v, (value.T if turn else value).astype(BF16))
                return carry

            lax.fori_loop(0, terms // group, body, 0)

        @pl.when(ahead)
        def _():
            run(True)

        @pl.when(jnp.logical_not(ahead))
        def _():
            run(False)

    def load_wait(slot):
        load(left_hbm, slot).wait()

    def slow_copy(k):
        return pltpu.make_async_remote_copy(
            src_ref=out_slow.at[k], dst_ref=slow.at[k],
            send_sem=slow_send.at[k], recv_sem=slow_recv.at[k],
            device_id={"region": slow_peer}, device_id_type=MESH,
        )

    load_wait(0)
    mix(env.at[0], frame.at[1])
    (start_norm,) = scalar_finish(0, 1)
    rescale = sectors * width / start_norm

    def store_slow(v, value):
        for k in range(slabs):
            out_slow[k, v] = value[k * rows : (k + 1) * rows]

    norms[0] = jnp.broadcast_to(rescale, (8, 128))
    pair_copy(2, norms.at[0], norms.at[1]).start()
    carry_env(frame.at[0], even, rescale, store_slow)

    @pl.when(inner)
    def _():
        for k in range(slabs):
            slow_copy(k).start()

    def store_fast(v, value):
        fast[v] = value

    pair_copy(0, frame.at[1], peer_frame.at[0]).wait_recv()
    pair_copy(1, left_hbm, raw).wait_recv()
    peer_frame[1] = nt(unit[...], peer_frame[0]).astype(BF16)
    mix(raw, peer_frame.at[1])
    pair_copy(2, norms.at[0], norms.at[1]).wait_recv()
    carry_env(peer_frame.at[0], jnp.logical_not(even), norms[1][0:1, 0:1], store_fast)

    @pl.when(jnp.logical_and(edge, even))
    def _():
        load_wait(1)

        def body(v, carry):
            for k in range(slabs):
                slow[k, v] = env[1, v, k * rows : (k + 1) * rows, :]
            return carry

        lax.fori_loop(0, terms, body, 0)

    @pl.when(jnp.logical_and(edge, jnp.logical_not(even)))
    def _():
        load_wait(1)

        def body(v, carry):
            value = nt(unit[...], env[1, v]).astype(BF16)
            for k in range(slabs):
                slow[k, v] = value[k * rows : (k + 1) * rows]
            return carry

        lax.fori_loop(0, terms, body, 0)

    vec[0] = (frame[0].astype(F32) * jnp.sqrt(cells / start_norm)).astype(BF16)
    diag = diag_ref[...]
    diag_frame = jnp.where(even, diag, nt(unit[...], diag).astype(BF16))
    inv_root = 1.0 / math.sqrt(terms)

    def y_copy(it, k, d):
        peer_y = lax.rem(my_y + d, ys)
        return pltpu.make_async_remote_copy(
            src_ref=part[it].at[k, peer_y], dst_ref=y_in[it].at[k, d - 1],
            send_sem=y_send.at[it, k, d - 1], recv_sem=y_recv.at[it, k, d - 1],
            device_id={"sector": my_z * ys + peer_y}, device_id_type=MESH,
        )

    def z_copy(it, k, d):
        peer_z = lax.rem(my_z + d, zs)
        return pltpu.make_async_remote_copy(
            src_ref=zsum[it].at[k, peer_z], dst_ref=z_in[it].at[k, d - 1],
            send_sem=z_send.at[it, k, d - 1], recv_sem=z_recv.at[it, k, d - 1],
            device_id={"sector": peer_z * ys + my_y}, device_id_type=MESH,
        )

    def z_phase(it, k):
        for d in range(1, ys):
            y_copy(it, k, d).wait_recv()
        added = part[it][k, my_y].astype(F32)
        for d in range(1, ys):
            added = added + y_in[it][k, d - 1].astype(F32)
        zsum[it][k] = added.astype(BF16)
        for d in range(1, zs):
            z_copy(it, k, d).start()

    def apply(it):
        merge = slabs // SLABS[it]
        tile = merge * rows

        lag = LAGS[it]

        def body(k, carry):
            if it == 0:
                @pl.when(inner)
                def _():
                    slow_copy(k).wait_recv()

            left = slow[pl.ds(k * merge, merge)].reshape(merge * terms * rows, width)
            half = nn(left, vec[it]).astype(BF16)
            for w in range(terms):
                pieces = [
                    half[(j * terms + w) * rows : (j * terms + w + 1) * rows] for j in range(merge)
                ]
                term[w, 0:tile, :] = nn(jnp.concatenate(pieces, axis=0), fast[w]).astype(BF16)
            matrix = route[...]
            for i in range(tile // 16):
                piece = term[:, 16 * i : 16 * i + 16, :].reshape(tall, width)
                both = (nn(matrix, piece) * inv_root).astype(BF16).reshape(ys, zs, 16, width)
                part[it][k, :, :, 16 * i : 16 * i + 16, :] = both
            for d in range(1, ys):
                y_copy(it, k, d).start()

            @pl.when(k >= lag)
            def _():
                z_phase(it, k - lag)

            return carry

        lax.fori_loop(0, SLABS[it], body, 0)
        for k in range(SLABS[it] - lag, SLABS[it]):
            z_phase(it, k)
        for k in range(SLABS[it]):
            for d in range(1, zs):
                z_copy(it, k, d).wait_recv()
            added = zsum[it][k, my_z].astype(F32)
            for d in range(1, zs):
                added = added + z_in[it][k, d - 1].astype(F32)
            result[it, k * tile : (k + 1) * tile, :] = added
        source = vec[it].astype(F32)
        value = jnp.where(keep, result[it] + diag_frame.astype(F32) * source, 0.0)
        result[it] = value

    apply(0)
    first = result[0]
    vec[1] = first.astype(BF16)
    start = vec[0].astype(F32)
    scalar_start(1, [total(start * start), total(start * first), total(first * first)])
    apply(1)
    vv, vh, hh = scalar_finish(1, 3)
    energy = vh / vv
    near = 1.0 + STEP * energy
    scale = jnp.sqrt(cells / jnp.maximum(near * near * vv - 2.0 * STEP * near * vh + STEP * STEP * hh, vv))
    start = vec[0].astype(F32)
    first = result[0]
    x = scale * near * start - scale * STEP * first
    applied = scale * near * first - scale * STEP * result[1]
    y = applied - energy * x
    result[0] = x
    result[1] = y
    scalar_start(2, [total(x * x), total(x * y), total(y * y)])
    xx, xy, yy = scalar_finish(2, 3)
    gap = xy / xx
    norm = xx + STEP * STEP * jnp.maximum(yy - gap * xy, 0.0)
    grow = jnp.sqrt(cells / norm)
    bond = (grow * (result[0] - STEP * (result[1] - gap * result[0]))).astype(BF16)

    @pl.when(even)
    def _():
        bond_ref[...] = bond

    @pl.when(jnp.logical_not(even))
    def _():
        bond_ref[...] = nt(unit[...], bond).astype(BF16)

    energy_ref[...] = jnp.broadcast_to(energy + gap, (1, 128))

    for which in range(3):
        for d in range(1, sectors):
            scalar_copy(which, d).wait_send()
    pair_copy(0, frame.at[1], peer_frame.at[0]).wait_send()
    pair_copy(1, left_hbm, raw).wait_send()
    pair_copy(2, norms.at[0], norms.at[1]).wait_send()

    @pl.when(inner)
    def _():
        for k in range(slabs):
            slow_copy(k).wait_send()

    for it in range(ITERS):
        for k in range(SLABS[it]):
            for d in range(1, ys):
                y_copy(it, k, d).wait_send()
            for d in range(1, zs):
                z_copy(it, k, d).wait_send()


def local(regions, ys, zs, psi, left_env, right_env, diagonal, lc, rc, mask, target, size):
    width, terms = psi.shape[-1], left_env.shape[2]
    sectors, slabs = ys * zs, SLABS[0]
    rows, tiles = width // slabs, [width // n for n in SLABS]
    y_peers, z_peers = max(ys - 1, 1), max(zs - 1, 1)
    envs = (terms, width, width)
    vmem = pl.BlockSpec(memory_space=pltpu.VMEM)
    smem = pl.BlockSpec(memory_space=pltpu.SMEM)
    hbm = pl.BlockSpec(memory_space=pl.ANY)
    dma = pltpu.SemaphoreType.DMA
    bond, energy = pl.pallas_call(
        functools.partial(kernel, regions, ys, zs, width, terms),
        out_shape=(
            jax.ShapeDtypeStruct((width, width), BF16),
            jax.ShapeDtypeStruct((1, 128), F32),
        ),
        in_specs=[vmem, hbm, hbm, vmem, vmem, vmem, vmem, smem, smem],
        out_specs=(vmem, vmem),
        scratch_shapes=[
            pltpu.VMEM((2,) + envs, BF16),
            pltpu.VMEM(envs, BF16),
            pltpu.VMEM((2, width, width), BF16),
            pltpu.VMEM((2, width, width), BF16),
            pltpu.VMEM(envs, BF16),
            pltpu.VMEM((2, 8, 128), F32),
            pltpu.VMEM((slabs, terms, rows, width), BF16),
            pltpu.VMEM((slabs, terms, rows, width), BF16),
            pltpu.VMEM(envs, BF16),
            pltpu.VMEM((2, width, width), BF16),
            pltpu.VMEM((width, width), BF16),
            pltpu.VMEM((sectors * 16, terms * 16), BF16),
            pltpu.VMEM((terms, max(tiles), width), BF16),
            *[pltpu.VMEM((n, ys, zs, width // n, width), BF16) for n in SLABS],
            *[pltpu.VMEM((n, y_peers, zs, width // n, width), BF16) for n in SLABS],
            *[pltpu.VMEM((n, zs, width // n, width), BF16) for n in SLABS],
            *[pltpu.VMEM((n, z_peers, width // n, width), BF16) for n in SLABS],
            pltpu.VMEM((2, width, width), F32),
            pltpu.VMEM((3, sectors, 8, 128), F32),
            dma((2,)),
            dma((slabs,)),
            dma((slabs,)),
            dma((3,)),
            dma((3,)),
            dma((ITERS, slabs, y_peers)),
            dma((ITERS, slabs, y_peers)),
            dma((ITERS, slabs, z_peers)),
            dma((ITERS, slabs, z_peers)),
            dma((3, sectors - 1)),
            dma((3, sectors - 1)),
        ],
        compiler_params=pltpu.CompilerParams(
            collective_id=0, has_side_effects=True, vmem_limit_bytes=56 * 2**20
        ),
    )(
        psi.reshape(width, width), left_env.reshape(envs), right_env.reshape(envs),
        diagonal.reshape(width, width), lc, rc, mask, target, size,
    )
    return bond.reshape(1, 1, width, width), energy[0, :1]


def solution(mesh):
    regions, sectors = mesh.shape["region"], mesh.shape["sector"]
    ys = 1
    while (2 * ys) * (2 * ys) * 2 <= sectors:
        ys *= 2
    in_specs = (
        P("region", "sector", None, None),
        P("region", "sector", None, None, None),
        P("region", "sector", None, None, None),
        P("region", "sector", None, None),
        P(),
        P(),
        P(),
        P("sector", None),
        P("sector"),
    )
    out_specs = (P("region", "sector", None, None), P("region"))
    body = functools.partial(local, regions, ys, sectors // ys)
    return jax.shard_map(body, mesh=mesh, in_specs=in_specs, out_specs=out_specs, check_vma=False)
```
